128 devices in a mesh: ctx: 32 (over x, z, y_hi), tp: 4 (over y_lo, core).
Axes of the slice: x: 4, y: 4 (y_hi: 2, y_lo: 2; y = y_hi * 2 + y_lo), z: 4, core: 2. Of those that a mesh axis runs over, the one named last changes fastest.
Arguments:
- queries: bfloat16 [8192, 4096], P('ctx', 'tp'), may hold values from -6 to 6
- keys: bfloat16 [8192, 512], P('ctx', 'tp'), may hold values from -5.5 to 5.5
- values: bfloat16 [8192, 512], P('ctx', 'tp'), may hold values from -6 to 6
- prior_keys: bfloat16 [8192, 512], P('ctx', 'tp'), may hold values from -6 to 6
- prior_values: bfloat16 [8192, 512], P('ctx', 'tp'), may hold values from -6 to 6
- out_weight: bfloat16 [4096, 8192], P(None, 'tp'), may hold values from -0.09375 to 0.09375
- ssm_x: bfloat16 [8192, 8192], P('ctx', 'tp'), may hold values from -6 to 6
- ssm_bc: bfloat16 [8192, 2, 1024], P('ctx', None, 'tp'), may hold values from -6 to 6
- gate_z: bfloat16 [8192, 8192], P('ctx', 'tp'), may hold values from -6 to 6
- conv_x: float32 [4, 8192], P(None, 'tp'), may hold values from -3 to 3
- conv_bc: float32 [4, 2, 1024], P(None, None, 'tp'), may hold values from -3 to 3
- conv_prior_x: bfloat16 [3, 8192], P(None, 'tp'), may hold values from -12 to 12
- conv_prior_bc: bfloat16 [3, 2, 1024], P(None, None, 'tp'), may hold values from -6 to 6
- step_dt: float32 [8192, 128], P('ctx', 'tp'), may hold values from 0.01 to 0.1
- log_decay: float32 [8192, 128], P('ctx', 'tp')
- skip_d: float32 [128], P('tp'), may hold values from 0.5 to 1.5
- ssm_prior: float32 [128, 64, 256], P('tp'), may hold values from -6 to 6
- norm_gain: float32 [8192], P('tp'), may hold values from 0.5 to 1.5
Outputs:
- attn_out: bfloat16 [8192, 8192], P('ctx', 'tp')
- ssm_out: bfloat16 [8192, 8192], P('ctx', 'tp')
The draws below stay inside these ranges and needn't reach their ends.
All inputs are finite; a program needn't handle non-finite values.
Results may differ from the reference program's by a relative error of at most 0.017.
Values may be sent and summed in bfloat16 or wider, within the bound.
A program may use at most 320 MiB of HBM per device.

```python
import math
import jax
import jax.numpy as jnp
from jax import lax

D = 8192
QH = 32
KVH = 4
HD = 128
HALF_SSM_HEADS = 128
P_SIZE = 64
N = 256
GROUPS = 4
KCONV = 4
BLOCK = 256
TOK_DEV = 256
BLOCK_TOKENS = 8192
PRIOR = 8192
INNER = 8192


def draw_queries(key, part):
    key = jax.random.fold_in(key, 11)
    base = jnp.clip(jax.random.normal(key, (BLOCK_TOKENS, QH * HD), jnp.float32), -5.5, 5.5)
    return base.astype(jnp.bfloat16)


def draw_prior_keys(key, part):
    key = jax.random.fold_in(key, 12)
    base = jnp.clip(jax.random.normal(key, (PRIOR, KVH * HD), jnp.float32), -5.5, 5.5)
    return base.astype(jnp.bfloat16)


def draw_log_decay(key, part):
    key = jax.random.fold_in(key, 13)
    gathered_keys = jax.random.split(key, 7)
    slow_share = 0.5
    slow = jax.random.bernoulli(gathered_keys[0], slow_share, (HALF_SSM_HEADS,))
    slow_rate = jnp.exp(jax.random.uniform(gathered_keys[1], (HALF_SSM_HEADS,), jnp.float32, jnp.log(0.1), jnp.log(0.6))) / BLOCK_TOKENS
    fast_rate = jnp.exp(jax.random.uniform(gathered_keys[2], (HALF_SSM_HEADS,), jnp.float32, jnp.log(1.0 / 50.0), jnp.log(1.0 / 20.0)))
    decay_rate = jnp.where(slow, slow_rate, fast_rate)
    random_noise = jnp.exp(jax.random.uniform(gathered_keys[3], (BLOCK_TOKENS, HALF_SSM_HEADS), jnp.float32, jnp.log(0.5), jnp.log(2.0)))
    count = (BLOCK_TOKENS + 63) // 64
    region = jnp.exp(jax.random.uniform(gathered_keys[4], (count, HALF_SSM_HEADS), jnp.float32, jnp.log(0.6), jnp.log(1.6)))
    section_rows = region[jnp.arange(BLOCK_TOKENS) // 64]
    spike_locations = jax.random.randint(gathered_keys[5], (2,), 0, BLOCK_TOKENS)
    objective_value = jax.random.uniform(gathered_keys[6], (2, HALF_SSM_HEADS), jnp.float32, 0.2, 0.5)
    token_positions = jnp.arange(BLOCK_TOKENS)
    spike_amount = jnp.zeros((BLOCK_TOKENS, HALF_SSM_HEADS), jnp.float32)
    for index_value in range(2):
        spike_amount = spike_amount + jnp.where((token_positions == spike_locations[index_value])[:, None], jnp.log(1.0 - objective_value[index_value])[None, :], 0.0)
    return (-decay_rate[None, :] * random_noise * section_rows + spike_amount).astype(jnp.float32)


def level_of(rng, dims, shards, least, top_value):
    def one(dim, shards_of):
        steps = jax.random.uniform(jax.random.fold_in(jax.random.fold_in(rng, 6), dim), (shards_of,), jnp.float32, least / len(shards), top_value / len(shards))
        return jnp.repeat(jnp.exp(steps), dims[dim] // shards_of).reshape((-1,) + (1,) * (len(dims) - dim - 1))

    factor_of = one(*shards[0])
    for cut in shards[1:]:
        factor_of = factor_of * one(*cut)
    return factor_of


def centred(own_key, extent, spread, reach, pieces=(), kind=jnp.bfloat16):
    values = spread * jax.random.normal(own_key, extent, jnp.float32)
    if pieces:
        values = values * level_of(own_key, extent, pieces, -0.22, 0.18)
    return jnp.clip(values, -reach, reach).astype(kind)


def setup_inputs(seed: int = 0) -> dict:
    seeds = jax.random.split(jax.random.key(seed), 19)
    queries = draw_queries(jax.random.fold_in(seeds[18], 71), 0)
    keys = centred(seeds[1], (BLOCK_TOKENS, KVH * HD), 1.0, 5.5, ((0, 32), (1, 4)))
    values = centred(seeds[2], (BLOCK_TOKENS, KVH * HD), 1.0, 6.0, ((0, 32), (1, 4)))
    prior_keys = draw_prior_keys(jax.random.fold_in(seeds[18], 71), 0)
    prior_values = centred(seeds[4], (PRIOR, KVH * HD), 1.0, 6.0, ((0, 32), (1, 4)))
    out_weight = centred(seeds[5], (QH * HD, D), (QH * HD) ** -0.5, 0.09375, ((1, 4),))
    ssm_x = centred(seeds[6], (BLOCK_TOKENS, INNER), 1.0, 6.0, ((0, 32), (1, 4)))
    ssm_bc = centred(seeds[7], (BLOCK_TOKENS, 2, GROUPS * N), 1.0, 6.0, ((0, 32), (2, 4)))
    gate_z = centred(seeds[8], (BLOCK_TOKENS, INNER), 1.0, 6.0, ((0, 32), (1, 4)))
    conv_x = centred(seeds[9], (KCONV, INNER), KCONV ** -0.5, 3.0, ((1, 4),), jnp.float32)
    conv_bc = centred(seeds[10], (KCONV, 2, GROUPS * N), KCONV ** -0.5, 3.0, ((2, 4),), jnp.float32)
    conv_prior_x = centred(seeds[11], (KCONV - 1, INNER), 3.0, 12.0, ((1, 4),))
    conv_prior_bc = centred(seeds[12], (KCONV - 1, 2, GROUPS * N), 1.0, 6.0, ((2, 4),))
    step_dt = jnp.clip(jnp.exp(math.log(0.1) - 2.3025851 * jax.random.uniform(seeds[13], (BLOCK_TOKENS, HALF_SSM_HEADS), jnp.float32) ** level_of(seeds[13], (BLOCK_TOKENS, HALF_SSM_HEADS), ((0, 32), (1, 4)), -0.2, 0.2)), 0.01, 0.1)
    log_decay = draw_log_decay(jax.random.fold_in(seeds[18], 71), 0)
    skip_d = jnp.clip(0.5 + 1.0 * jax.random.uniform(seeds[15], (HALF_SSM_HEADS,), jnp.float32) ** level_of(seeds[15], (HALF_SSM_HEADS,), ((0, 4),), -0.2, 0.2), 0.5, 1.5)
    ssm_prior = centred(seeds[16], (HALF_SSM_HEADS, P_SIZE, N), 1.0, 6.0, ((0, 4),), jnp.float32)
    norm_gain = jnp.clip(1.0 + 0.1 * jax.random.normal(seeds[17], (INNER,), jnp.float32), 0.5, 1.5)
    return {"queries": queries, "keys": keys, "values": values, "prior_keys": prior_keys, "prior_values": prior_values, "out_weight": out_weight, "ssm_x": ssm_x, "ssm_bc": ssm_bc, "gate_z": gate_z, "conv_x": conv_x, "conv_bc": conv_bc, "conv_prior_x": conv_prior_x, "conv_prior_bc": conv_prior_bc, "step_dt": step_dt, "log_decay": log_decay, "skip_d": skip_d, "ssm_prior": ssm_prior, "norm_gain": norm_gain}


def ssd_block(state, xb, bb, cb, dtb, ldb):
    length = ldb.shape[0]
    cum = jnp.cumsum(ldb, axis=0)
    diff = cum[:, None, :] - cum[None, :, :]
    lower = (jnp.arange(length, dtype=jnp.int32)[:, None] >= jnp.arange(length, dtype=jnp.int32)[None, :])[:, :, None]
    decay = jnp.where(lower, jnp.exp(jnp.where(lower, diff, 0.0)), 0.0)
    inner = jnp.dot(cb, bb.T, precision=lax.Precision.HIGHEST)
    mixing = inner[:, :, None] * decay * dtb[None, :, :]
    y_block = jnp.einsum('tsh,shp->thp', mixing, xb, precision=lax.Precision.HIGHEST)
    y_block = y_block + jnp.exp(cum)[:, :, None] * jnp.einsum('tn,hpn->thp', cb, state, precision=lax.Precision.HIGHEST)
    carried = jnp.exp(cum[-1:] - cum) * dtb
    state = jnp.exp(cum[-1])[:, None, None] * state + jnp.einsum('shp,sn->hpn', carried[:, :, None] * xb, bb, precision=lax.Precision.HIGHEST)
    return (state, y_block)

def causal_conv(prior, current, taps):
    extended = jnp.concatenate([prior, current], axis=0).astype(jnp.float32)
    length = current.shape[0]
    total = taps[0] * extended[0:length]
    for tap in range(1, taps.shape[0]):
        total = total + taps[tap] * extended[tap:tap + length]
    return jax.nn.silu(total)

def reference(queries, keys, values, prior_keys, prior_values, out_weight, ssm_x, ssm_bc, gate_z, conv_x, conv_bc, conv_prior_x, conv_prior_bc, step_dt, log_decay, skip_d, ssm_prior, norm_gain):
    group_q = QH // KVH
    all_keys = jnp.concatenate([prior_keys, keys], axis=0)
    all_values = jnp.concatenate([prior_values, values], axis=0)
    key_pos = jnp.arange(PRIOR + BLOCK_TOKENS, dtype=jnp.int32) - PRIOR
    scale = HD ** (-0.5)
    blocks_q = BLOCK_TOKENS // TOK_DEV

    def attend_block(index_value):
        block = index_value // KVH
        group = index_value % KVH
        query_block = lax.dynamic_slice(queries, (block * TOK_DEV, group * group_q * HD), (TOK_DEV, group_q * HD))
        query_block = query_block.reshape(TOK_DEV, group_q, HD).astype(jnp.float32)
        key_block = lax.dynamic_slice_in_dim(all_keys, group * HD, HD, 1).astype(jnp.float32)
        value_block = lax.dynamic_slice_in_dim(all_values, group * HD, HD, 1).astype(jnp.float32)
        scores = jnp.einsum('thd,sd->hts', query_block, key_block, precision=lax.Precision.HIGHEST) * scale
        query_pos = block * TOK_DEV + jnp.arange(TOK_DEV, dtype=jnp.int32)
        allowed = (key_pos[None, :] <= query_pos[:, None])[None, :, :]
        scores = jnp.where(allowed, scores, -1e+30)
        top = lax.optimization_barrier(jnp.max(scores, axis=-1, keepdims=True))
        weights = jnp.where(allowed, jnp.exp(scores - top), 0.0)
        totals = lax.optimization_barrier(jnp.sum(weights, axis=-1))
        rounded = lax.optimization_barrier(weights.astype(jnp.bfloat16)).astype(jnp.float32)
        heads = jnp.einsum('hts,sd->htd', rounded, value_block, precision=lax.Precision.HIGHEST) / totals[:, :, None]
        return heads.transpose(1, 0, 2).reshape(TOK_DEV, group_q * HD)
    stacked = lax.map(attend_block, jnp.arange(blocks_q * KVH, dtype=jnp.int32))
    attn_heads = stacked.reshape(blocks_q, KVH, TOK_DEV, group_q * HD).transpose(0, 2, 1, 3).reshape(BLOCK_TOKENS, QH * HD).astype(jnp.bfloat16)
    attn_out = jnp.dot(attn_heads, out_weight, preferred_element_type=jnp.float32).astype(jnp.bfloat16)
    conv_inner = causal_conv(conv_prior_x, ssm_x, conv_x)
    conv_proj = causal_conv(conv_prior_bc, ssm_bc, conv_bc)
    heads_group = HALF_SSM_HEADS // GROUPS
    blocks_s = BLOCK_TOKENS // BLOCK
    x_heads = conv_inner.reshape(BLOCK_TOKENS, HALF_SSM_HEADS, P_SIZE)
    x_blocks = x_heads.reshape(blocks_s, BLOCK, GROUPS, heads_group, P_SIZE)
    b_blocks = conv_proj[:, 0].reshape(blocks_s, BLOCK, GROUPS, N)
    c_blocks = conv_proj[:, 1].reshape(blocks_s, BLOCK, GROUPS, N)
    dt_blocks = step_dt.reshape(blocks_s, BLOCK, GROUPS, heads_group)
    ld_blocks = log_decay.reshape(blocks_s, BLOCK, GROUPS, heads_group)
    group_block = jax.vmap(ssd_block, in_axes=(0, 1, 1, 1, 1, 1), out_axes=(0, 1))

    def advance(state, items):
        return group_block(state, items[0], items[1], items[2], items[3], items[4])
    start_state = ssm_prior.reshape(GROUPS, heads_group, P_SIZE, N)
    unused, y_blocks = lax.scan(advance, start_state, (x_blocks, b_blocks, c_blocks, dt_blocks, ld_blocks))
    mixed = y_blocks.reshape(BLOCK_TOKENS, HALF_SSM_HEADS, P_SIZE) + skip_d[None, :, None] * x_heads
    gated = mixed.reshape(BLOCK_TOKENS, INNER) * jax.nn.silu(gate_z.astype(jnp.float32))
    grouped = gated.reshape(BLOCK_TOKENS, GROUPS, INNER // GROUPS)
    normed = grouped * lax.rsqrt(lax.optimization_barrier(jnp.mean(grouped * grouped, axis=-1, keepdims=True)) + 1e-05)
    ssm_out = (normed.reshape(BLOCK_TOKENS, INNER) * norm_gain).astype(jnp.bfloat16)
    return (attn_out, ssm_out)
```

```python
import functools

import jax
import jax.numpy as jnp
from jax import lax
from jax.experimental import pallas as pl
from jax.experimental.pallas import tpu as pltpu
from jax.sharding import PartitionSpec as P

MESH = pl.DeviceIdType.MESH
F32 = jnp.float32
BF16 = jnp.bfloat16
HD = 128
CTX = 32
TP = 4
ROWS = 256
HEADS = 8
SH = 32
WIDE = 2048
PAIRS = 16
NSTATE = 256
MSG = 80
COEF = 1.4426950408889634 / (HD**0.5)
NT = (((1,), (1,)), ((), ()))
TN = (((0,), (0,)), ((), ()))


def dot(a, b, dims=(((1,), (0,)), ((), ()))):
    return lax.dot_general(a, b, dims, preferred_element_type=F32)


def exact_dot(a, b, dims):
    return lax.dot_general(
        a, b, dims, preferred_element_type=F32, precision=lax.Precision.HIGHEST
    )


def silu(v):
    return v / (1.0 + jnp.exp(-v))


def neighbour(c, dim, step):
    if dim == 0:
        return lax.rem(c + 8 * step + 32, 32)
    z = lax.rem(lax.div(c, 2), 4)
    return c + 2 * (lax.rem(z + step + 4, 4) - z)


def slot_of(c):
    return lax.div(c, 8) * 8 + lax.rem(c, 2) * 4 + lax.rem(lax.div(c, 2), 4)


def kernel(
    q_ref,
    k_ref,
    v_ref,
    pk_ref,
    pv_ref,
    w_hbm,
    x_ref,
    bc_ref,
    z_ref,
    taps_x,
    taps_bc,
    prior_x,
    prior_bc,
    dt_ref,
    ld_ref,
    skip_ref,
    prior_hbm,
    gain_ref,
    attn_ref,
    ssm_ref,
    kvb,
    acc,
    top,
    heads,
    w_ref,
    edge_x,
    edge_bc,
    ext,
    ext_bc,
    b_ref,
    c_ref,
    g_ref,
    aux,
    cum_t,
    xa,
    msg,
    got,
    state,
    back,
    incoming,
    squares,
    bar_unused,
    w_sem,
    prior_sem,
    y_send,
    y_recv,
    kv_send,
    kv_recv,
    edge_send,
    edge_recv,
    st_send,
    st_recv,
    in_send,
    in_recv,
    hd_send,
    hd_recv,
):
    c = lax.axis_index("ctx")
    t = lax.axis_index("tp")
    mate = c + 1 - 2 * lax.rem(c, 2)

    def remote(src, dst, send, recv, dev):
        return pltpu.make_async_remote_copy(
            src_ref=src,
            dst_ref=dst,
            send_sem=send,
            recv_sem=recv,
            device_id=dev,
            device_id_type=MESH,
        )

    w_copy = pltpu.make_async_copy(w_hbm, w_ref, w_sem)
    w_copy.start()
    prior_copy = pltpu.make_async_copy(
        prior_hbm.at[pl.ds(pl.multiple_of(c * 64, 64), 64)], state, prior_sem
    )
    prior_copy.start()
    own = slot_of(c)
    kvb[own, 0] = k_ref[...]
    kvb[own, 1] = v_ref[...]
    kvb[own, 2] = pk_ref[...]
    kvb[own, 3] = pv_ref[...]

    barrier = pltpu.get_barrier_semaphore()

    def greet_ctx(i, carry):
        pl.semaphore_signal(
            barrier, inc=1, device_id=(lax.rem(c + i, CTX), t), device_id_type=MESH
        )
        return carry

    def greet_tp(i, carry):
        pl.semaphore_signal(
            barrier, inc=1, device_id=(c, lax.rem(t + i, TP)), device_id_type=MESH
        )
        return carry

    lax.fori_loop(1, CTX, greet_ctx, 0)
    lax.fori_loop(1, TP, greet_tp, 0)
    pl.semaphore_wait(barrier, CTX - 1 + TP - 1)

    def first(half):
        return 0 if half == 0 else 1

    def piece(slot, half, quarter):
        if quarter is None:
            return kvb.at[slot, pl.ds(2 * half, 2)]
        return kvb.at[slot, 2 * half + quarter]

    def kv_copy(chunk, half, quarter, send, dest):
        slot = slot_of(chunk)
        ref = piece(slot, half, quarter)
        recv = kv_recv.at[slot, half, 0 if quarter is None else quarter]
        return remote(ref, ref, send, recv, (dest, t))

    def base(p):
        return c if p == 0 else mate

    def send_desc(kind, p, r, half, way):
        dim1, dim2 = first(half), 1 - first(half)
        step = 1 - 2 * way
        if kind == "p1a":
            return kv_copy(
                base(p), half, None, kv_send.at[p, 0, half, way], neighbour(c, dim1, step)
            )
        if kind == "p1b":
            chunk = neighbour(base(p), dim1, -step)
            return kv_copy(
                chunk, half, way, kv_send.at[p, 1, half, way], neighbour(c, dim1, step)
            )
        row = neighbour(base(p), dim1, r)
        if kind == "p2a":
            return kv_copy(
                row, half, None, kv_send.at[p, 2 + r, half, way], neighbour(c, dim2, step)
            )
        chunk = neighbour(row, dim2, -step)
        return kv_copy(
            chunk, half, way, kv_send.at[p, 6 + r, half, way], neighbour(c, dim2, step)
        )

    def wait_whole(chunk, half):
        kv_copy(chunk, half, None, kv_send.at[0, 0, 0, 0], c).wait_recv()

    def wait_split(chunk, half):
        for quarter in range(2):
            kv_copy(chunk, half, quarter, kv_send.at[0, 0, 0, 0], c).wait_recv()

    def each(fn):
        for half in range(2):
            for way in range(2):
                fn(half, way)

    def stage_a(p):
        each(lambda half, way: send_desc("p1a", p, 0, half, way).start())
        each(lambda half, way: send_desc("p2a", p, 0, half, way).start())

    def stage_b(p):
        def got_one(half, way):
            wait_whole(neighbour(base(p), first(half), 2 * way - 1), half)
            send_desc("p1b", p, 0, half, way).start()

        each(got_one)
        for r in (1, 3):
            each(lambda half, way: send_desc("p2a", p, r, half, way).start())

    def stage_c(p):
        for half in range(2):
            wait_split(neighbour(base(p), first(half), 2), half)
        each(lambda half, way: send_desc("p2a", p, 2, half, way).start())
        forward(p, 0)

    def forward(p, r):
        def got_one(half, way):
            row = neighbour(base(p), first(half), r)
            wait_whole(neighbour(row, 1 - first(half), 2 * way - 1), half)
            send_desc("p2b", p, r, half, way).start()

        each(got_one)

    def stage_d(p):
        forward(p, 1)
        forward(p, 3)

    def stage_e(p):
        forward(p, 2)

    def stage_f(p):
        def one(r, carry):
            for half in range(2):
                row = neighbour(base(p), first(half), r)
                wait_split(neighbour(row, 1 - first(half), 2), half)
            return carry

        lax.fori_loop(0, 4, one, 0)

    y_copy = remote(kvb.at[own], kvb.at[own], y_send, y_recv, (mate, t))
    y_got = remote(kvb.at[slot_of(mate)], kvb.at[slot_of(mate)], y_send, y_recv, (mate, t))

    following = lax.rem(c + 1, CTX)
    edge_copies = [
        remote(x_ref.at[pl.ds(ROWS - 16, 16)], edge_x, edge_send.at[0], edge_recv.at[0], (following, t)),
        remote(bc_ref.at[pl.ds(ROWS - 16, 16)], edge_bc, edge_send.at[1], edge_recv.at[1], (following, t)),
    ]
    for copy in edge_copies:
        copy.start()
    y_copy.start()
    stage_a(0)

    row_i = lax.broadcasted_iota(jnp.int32, (ROWS, ROWS), 0)
    col_i = lax.broadcasted_iota(jnp.int32, (ROWS, ROWS), 1)
    lower = row_i >= col_i
    ones_low = jnp.where(lower, 1.0, 0.0).astype(F32)
    ld = ld_ref[...]
    cum = exact_dot(ones_low, ld, (((1,), (0,)), ((), ())))
    cum_t[...] = exact_dot(ld, ones_low, (((0,), (1,)), ((), ())))
    dt = dt_ref[...]
    aux[:, 0:32] = cum
    aux[:, 32:64] = dt
    aux[:, 64:96] = jnp.exp(cum[ROWS - 1 : ROWS] - cum) * dt
    aux[:, 96:128] = jnp.exp(cum)

    for copy in edge_copies:
        copy.wait_recv()

    at_start = c == 0

    def conv(buffer, edge, own_prior, here, taps):
        before = jnp.where(at_start, own_prior.astype(F32), edge.astype(F32)[8:16])
        buffer[0:8, :] = before
        buffer[8 : 8 + ROWS, :] = here.astype(F32)
        total = taps[0:1] * buffer[5 : 5 + ROWS, :]
        for k in range(1, 4):
            total = total + taps[k : k + 1] * buffer[5 + k : 5 + k + ROWS, :]
        return silu(total)

    proj = conv(ext_bc, edge_bc[...], prior_bc[...], bc_ref[...], taps_bc[...])
    b_ref[...] = proj[:, :NSTATE].astype(BF16)
    c_ref[...] = proj[:, NSTATE:].astype(BF16)
    g_ref[...] = dot(c_ref[...], b_ref[...], NT)

    left_half = lax.broadcasted_iota(jnp.int32, (ROWS, 128), 1) < 64

    def columns(pair):
        return pl.ds(pl.multiple_of(pair * 128, 128), 128)

    def rolled(pair):
        return pltpu.roll(aux[...], 128 - 2 * pair, 1)

    def spread(lanes, at):
        return jnp.where(left_half, lanes[:, at : at + 1], lanes[:, at + 1 : at + 2])

    def state_copy(h):
        return remote(msg.at[h], got.at[c], st_send.at[h], st_recv.at[c], (h, t))

    def local_states(pair, carry):
        cols = columns(pair)
        act = conv(ext, edge_x[:, cols], prior_x[:, cols], x_ref[:, cols], taps_x[:, cols])
        xa[:, cols] = act
        lanes = rolled(pair)
        weighted = (act * spread(lanes, 64)).astype(BF16)
        made = dot(weighted, b_ref[...], TN).astype(BF16)
        row = lax.broadcasted_iota(jnp.int32, (16, NSTATE), 0)
        for sub in range(2):
            h = 2 * pair + sub
            msg[h, 0:64, :] = made[64 * sub : 64 * sub + 64]
            total = jnp.broadcast_to(lanes[ROWS - 1 : ROWS, sub : sub + 1], (16, NSTATE))
            hi = total.astype(BF16).astype(F32)
            mid = (total - hi).astype(BF16).astype(F32)
            low = total - hi - mid
            parts = jnp.where(row == 0, hi, jnp.where(row == 1, mid, jnp.where(row == 2, low, 0.0)))
            msg[h, 64:80, :] = parts.astype(BF16)

            @pl.when(h != c)
            def _():
                state_copy(h).start()

            @pl.when(h == c)
            def _():
                got[c] = msg[h]

        @pl.when(pair == 6)
        def _():
            stage_b(0)

        @pl.when(pair == 12)
        def _():
            y_got.wait_recv()
            stage_a(1)

        return carry

    lax.fori_loop(0, PAIRS, local_states, 0)
    stage_c(0)

    def within_block(pair, carry):
        cols = columns(pair)
        lanes = rolled(pair)
        act = xa[:, cols]
        scaled = (act * spread(lanes, 32)).astype(BF16)
        parts = []
        for sub in range(2):
            h = 2 * pair + sub
            diff = lanes[:, sub : sub + 1] - cum_t[pl.ds(h, 1), :]
            decay = jnp.exp(jnp.where(lower, diff, -1e30))
            parts.append(dot((g_ref[...] * decay).astype(BF16), scaled))
        xa[:, cols] = jnp.where(left_half, parts[0], parts[1]) + skip_ref[:, cols] * act

        @pl.when(pair == 6)
        def _():
            stage_b(1)

        @pl.when(pair == 12)
        def _():
            stage_d(0)

        return carry

    lax.fori_loop(0, PAIRS, within_block, 0)
    stage_e(0)

    acc[...] = jnp.zeros_like(acc)
    top[...] = jnp.full(top.shape, -1e30, F32)

    def attend(h, keys, vals, allowed):
        query = q_ref[:, pl.ds(pl.multiple_of(h * HD, HD), HD)]
        scores = dot(query, keys, NT)
        if allowed is not None:
            scores = jnp.where(allowed, scores, -1e30)
        return scores

    def absorb(h, scores, vals):
        before = top[h]
        new = jnp.maximum(before, jnp.max(scores, axis=1, keepdims=True))
        top[h] = new
        shrink = jnp.exp2((before - new) * COEF)
        weights = jnp.exp2((scores - new[:, 0:1]) * COEF).astype(BF16)
        wide = jnp.concatenate([vals, jnp.ones_like(vals)], axis=1)
        acc[h] = acc[h] * jnp.concatenate([shrink, shrink], axis=1) + dot(weights, wide)

    def cached(g, carry):
        @pl.when(g == 1)
        def _():
            stage_c(1)

        @pl.when(g == 3)
        def _():
            stage_d(1)
            stage_e(1)

        @pl.when(g == 4)
        def _():
            stage_f(0)

        @pl.when(g == 7)
        def _():
            stage_f(1)

        plane = jnp.where((g == 3) | (g >= 5), 1, 0)
        far = jnp.where(
            (g == 0) | (g == 3), 0, jnp.where((g == 1) | (g == 5), 1, jnp.where((g == 2) | (g == 6), 3, 2))
        )
        x_at = lax.rem(lax.div(c, 8) + far, 4)
        y_at = lax.rem(lax.rem(c, 2) + plane, 2)
        slot = x_at * 8 + y_at * 4
        keys = kvb[pl.ds(slot, 4), 2].reshape(4 * ROWS, HD)
        vals = kvb[pl.ds(slot, 4), 3].reshape(4 * ROWS, HD)

        def two(i, carry2):
            s0 = attend(2 * i, keys, vals, None)
            s1 = attend(2 * i + 1, keys, vals, None)
            absorb(2 * i, s0, vals)
            absorb(2 * i + 1, s1, vals)
            return carry2

        lax.fori_loop(0, HEADS // 2, two, 0)
        return carry

    lax.fori_loop(0, 8, cached, 0)

    prior_copy.wait()

    def back_copy(j):
        here = pl.ds(pl.multiple_of(c * 64, 64), 64)
        return remote(back.at[j], incoming.at[here], in_send.at[j], in_recv.at[c], (j, t))

    def scan(j, carry):
        @pl.when(j != c)
        def _():
            remote(msg.at[j], got.at[j], st_send.at[j], st_recv.at[j], (j, t)).wait_recv()

        now = state[...]
        back[j] = now.astype(BF16)

        @pl.when(j != c)
        def _():
            back_copy(j).start()

        @pl.when(j == c)
        def _():
            incoming[pl.ds(pl.multiple_of(c * 64, 64), 64), :] = now.astype(BF16)

        tail = got[j, 64:80, :].astype(F32)
        total = tail[0:1] + tail[1:2] + tail[2:3]
        state[...] = jnp.exp(total) * now + got[j, 0:64, :].astype(F32)
        return carry

    lax.fori_loop(0, CTX, scan, 0)

    def head_copy(h, i):
        cols = pl.ds(pl.multiple_of((t * HEADS + h) * HD, HD), HD)
        return remote(
            heads.at[:, cols],
            heads.at[:, cols],
            hd_send.at[h, i],
            hd_recv.at[t, h],
            (c, lax.rem(t + i, TP)),
        )

    def head_block(h, carry):
        def whole(g, carry2):
            slot = g * 4
            keys = kvb[pl.ds(slot, 4), 0].reshape(4 * ROWS, HD)
            vals = kvb[pl.ds(slot, 4), 1].reshape(4 * ROWS, HD)
            absorb(h, attend(h, keys, vals, None), vals)
            return carry2

        lax.fori_loop(0, 2 * lax.div(c, 8), whole, 0)

        def single(j, carry2):
            slot = slot_of(j)
            vals = kvb[slot, 1]
            absorb(h, attend(h, kvb[slot, 0], vals, None), vals)
            return carry2

        lax.fori_loop(lax.div(c, 8) * 8, c, single, 0)
        vals = kvb[own, 1]
        absorb(h, attend(h, kvb[own, 0], vals, lower), vals)
        full = acc[h]
        cols = pl.ds(pl.multiple_of((t * HEADS + h) * HD, HD), HD)
        heads[:, cols] = (full[:, :HD] / full[:, HD:]).astype(BF16)
        for i in range(1, TP):
            head_copy(h, i).start()
        return carry

    lax.fori_loop(0, HEADS, head_block, 0)

    def in_wait(j, carry):
        @pl.when(j != c)
        def _():
            rows = pl.ds(pl.multiple_of(j * 64, 64), 64)
            remote(back.at[j], incoming.at[rows], in_send.at[j], in_recv.at[j], (j, t)).wait_recv()

        return carry

    lax.fori_loop(0, CTX, in_wait, 0)
    squares[...] = jnp.zeros_like(squares)

    def mix(pair, carry):
        cols = columns(pair)
        lanes = rolled(pair)
        earlier = dot(c_ref[...], incoming[cols, :], NT)
        mixed = xa[:, cols] + spread(lanes, 96) * earlier
        gated = mixed * silu(z_ref[:, cols].astype(F32))
        squares[...] += gated * gated
        xa[:, cols] = gated
        return carry

    lax.fori_loop(0, PAIRS, mix, 0)
    mean = jnp.sum(squares[...], axis=1, keepdims=True) * (1.0 / WIDE)
    squares[...] = jnp.broadcast_to(lax.rsqrt(mean + 1e-05), squares.shape)

    def norm(pair, carry):
        cols = columns(pair)
        ssm_ref[:, cols] = (xa[:, cols] * squares[...] * gain_ref[:, cols]).astype(BF16)
        return carry

    lax.fori_loop(0, PAIRS, norm, 0)

    def head_wait(h, carry):
        for i in range(1, TP):
            src = lax.rem(t + i, TP)
            cols = pl.ds(pl.multiple_of((src * HEADS + h) * HD, HD), HD)
            remote(
                heads.at[:, cols], heads.at[:, cols], hd_send.at[h, i], hd_recv.at[src, h], (c, src)
            ).wait_recv()
        return carry

    lax.fori_loop(0, HEADS, head_wait, 0)
    w_copy.wait()

    def project(n, carry):
        cols = pl.ds(pl.multiple_of(n * 256, 256), 256)
        attn_ref[:, cols] = dot(heads[...], w_ref[:, cols]).astype(BF16)
        return carry

    lax.fori_loop(0, WIDE // 256, project, 0)

    for copy in edge_copies:
        copy.wait_send()
    y_copy.wait_send()
    for p in range(2):
        each(lambda half, way: send_desc("p1a", p, 0, half, way).wait_send())
        each(lambda half, way: send_desc("p1b", p, 0, half, way).wait_send())

        def sent(r, carry):
            each(lambda half, way: send_desc("p2a", p, r, half, way).wait_send())
            each(lambda half, way: send_desc("p2b", p, r, half, way).wait_send())
            return carry

        lax.fori_loop(0, 4, sent, 0)

    def states_sent(j, carry):
        @pl.when(j != c)
        def _():
            state_copy(j).wait_send()
            back_copy(j).wait_send()

        return carry

    lax.fori_loop(0, CTX, states_sent, 0)

    def heads_sent(h, carry):
        for i in range(1, TP):
            head_copy(h, i).wait_send()
        return carry

    lax.fori_loop(0, HEADS, heads_sent, 0)


def per_device(
    queries,
    keys,
    values,
    prior_keys,
    prior_values,
    out_weight,
    ssm_x,
    ssm_bc,
    gate_z,
    conv_x,
    conv_bc,
    conv_prior_x,
    conv_prior_bc,
    step_dt,
    log_decay,
    skip_d,
    ssm_prior,
    norm_gain,
):
    vm = pl.BlockSpec(memory_space=pltpu.VMEM)
    anywhere = pl.BlockSpec(memory_space=pl.ANY)
    pad = ((5, 0), (0, 0))
    return pl.pallas_call(
        kernel,
        out_shape=(
            jax.ShapeDtypeStruct((ROWS, WIDE), BF16),
            jax.ShapeDtypeStruct((ROWS, WIDE), BF16),
        ),
        in_specs=[vm] * 5 + [anywhere] + [vm] * 10 + [anywhere, vm],
        out_specs=(vm, vm),
        scratch_shapes=[
            pltpu.VMEM((CTX, 4, ROWS, HD), BF16),
            pltpu.VMEM((HEADS, ROWS, 2 * HD), F32),
            pltpu.VMEM((HEADS, ROWS, HD), F32),
            pltpu.VMEM((ROWS, TP * HEADS * HD), BF16),
            pltpu.VMEM((TP * HEADS * HD, WIDE), BF16),
            pltpu.VMEM((16, WIDE), BF16),
            pltpu.VMEM((16, 2 * NSTATE), BF16),
            pltpu.VMEM((ROWS + 8, 128), F32),
            pltpu.VMEM((ROWS + 8, 2 * NSTATE), F32),
            pltpu.VMEM((ROWS, NSTATE), BF16),
            pltpu.VMEM((ROWS, NSTATE), BF16),
            pltpu.VMEM((ROWS, ROWS), F32),
            pltpu.VMEM((ROWS, 128), F32),
            pltpu.VMEM((SH, ROWS), F32),
            pltpu.VMEM((ROWS, WIDE), F32),
            pltpu.VMEM((SH, MSG, NSTATE), BF16),
            pltpu.VMEM((CTX, MSG, NSTATE), BF16),
            pltpu.VMEM((64, NSTATE), F32),
            pltpu.VMEM((CTX, 64, NSTATE), BF16),
            pltpu.VMEM((WIDE, NSTATE), BF16),
            pltpu.VMEM((ROWS, 128), F32),
            pltpu.VMEM((8, 128), F32),
            pltpu.SemaphoreType.DMA,
            pltpu.SemaphoreType.DMA,
            pltpu.SemaphoreType.DMA,
            pltpu.SemaphoreType.DMA,
            pltpu.SemaphoreType.DMA((2, 10, 2, 2)),
            pltpu.SemaphoreType.DMA((CTX, 2, 2)),
            pltpu.SemaphoreType.DMA((2,)),
            pltpu.SemaphoreType.DMA((2,)),
            pltpu.SemaphoreType.DMA((CTX,)),
            pltpu.SemaphoreType.DMA((CTX,)),
            pltpu.SemaphoreType.DMA((CTX,)),
            pltpu.SemaphoreType.DMA((CTX,)),
            pltpu.SemaphoreType.DMA((HEADS, TP)),
            pltpu.SemaphoreType.DMA((TP, HEADS)),
        ],
        compiler_params=pltpu.CompilerParams(
            collective_id=0, has_side_effects=True, vmem_limit_bytes=60 * 2**20
        ),
        name="hybrid",
    )(
        queries,
        keys,
        values,
        prior_keys,
        prior_values,
        out_weight,
        ssm_x,
        ssm_bc.reshape(ROWS, 2 * NSTATE),
        gate_z,
        conv_x,
        conv_bc.reshape(4, 2 * NSTATE),
        jnp.pad(conv_prior_x, pad),
        jnp.pad(conv_prior_bc.reshape(3, 2 * NSTATE), pad),
        step_dt,
        log_decay,
        jnp.repeat(skip_d, 64).reshape(1, WIDE),
        ssm_prior.reshape(WIDE, NSTATE),
        norm_gain.reshape(1, WIDE),
    )


def solution(mesh):
    in_specs = (
        P("ctx", "tp"),
        P("ctx", "tp"),
        P("ctx", "tp"),
        P("ctx", "tp"),
        P("ctx", "tp"),
        P(None, "tp"),
        P("ctx", "tp"),
        P("ctx", None, "tp"),
        P("ctx", "tp"),
        P(None, "tp"),
        P(None, None, "tp"),
        P(None, "tp"),
        P(None, None, "tp"),
        P("ctx", "tp"),
        P("ctx", "tp"),
        P("tp"),
        P("tp", None, None),
        P("tp"),
    )
    out_specs = (P("ctx", "tp"), P("ctx", "tp"))
    return jax.shard_map(
        per_device, mesh=mesh, in_specs=in_specs, out_specs=out_specs, check_vma=False
    )
```

```python
import functools

import jax
import jax.numpy as jnp
from jax import lax
from jax.experimental import pallas as pl
from jax.experimental.pallas import tpu as pltpu
from jax.sharding import PartitionSpec as P

MESH = pl.DeviceIdType.MESH
F32 = jnp.float32
BF16 = jnp.bfloat16
HD = 128
CTX = 32
TP = 4
ROWS = 256
HEADS = 8
SH = 32
WIDE = 2048
PAIRS = 16
NSTATE = 256
MSG = 80
GROUP = 8 * ROWS
COEF = 1.4426950408889634 / (HD**0.5)
NT = (((1,), (1,)), ((), ()))
TN = (((0,), (0,)), ((), ()))


def dot(a, b, dims=(((1,), (0,)), ((), ()))):
    return lax.dot_general(a, b, dims, preferred_element_type=F32)


def exact_dot(a, b, dims):
    return lax.dot_general(
        a, b, dims, preferred_element_type=F32, precision=lax.Precision.HIGHEST
    )


def silu(v):
    return v / (1.0 + jnp.exp(-v))


def neighbour(c, dim, step):
    if dim == 0:
        return lax.rem(c + 8 * step + 32, 32)
    z = lax.rem(lax.div(c, 2), 4)
    return c + 2 * (lax.rem(z + step + 4, 4) - z)


def slot_of(c):
    return lax.div(c, 8) * 8 + lax.rem(c, 2) * 4 + lax.rem(lax.div(c, 2), 4)


def kernel(
    q_ref,
    k_ref,
    v_ref,
    pk_ref,
    pv_ref,
    w_hbm,
    x_ref,
    bc_ref,
    z_ref,
    taps_x,
    taps_bc,
    prior_x,
    prior_bc,
    dt_ref,
    ld_ref,
    skip_ref,
    prior_hbm,
    gain_ref,
    attn_ref,
    ssm_ref,
    kvb,
    acc,
    top,
    heads,
    w_ref,
    edge_x,
    edge_bc,
    ext,
    ext_bc,
    b_ref,
    c_ref,
    g_ref,
    aux,
    cum_t,
    xa,
    msg,
    got,
    state,
    back,
    incoming,
    squares,
    w_sem,
    prior_sem,
    y_send,
    y_recv,
    kv_send,
    kv_recv,
    edge_send,
    edge_recv,
    st_send,
    st_recv,
    in_send,
    in_recv,
    hd_send,
    hd_recv,
):
    c = lax.axis_index("ctx")
    t = lax.axis_index("tp")
    mate = c + 1 - 2 * lax.rem(c, 2)

    def remote(src, dst, send, recv, dev):
        return pltpu.make_async_remote_copy(
            src_ref=src,
            dst_ref=dst,
            send_sem=send,
            recv_sem=recv,
            device_id=dev,
            device_id_type=MESH,
        )

    w_copy = pltpu.make_async_copy(w_hbm, w_ref, w_sem)
    w_copy.start()
    prior_copy = pltpu.make_async_copy(
        prior_hbm.at[pl.ds(pl.multiple_of(c * 64, 64), 64)], state, prior_sem
    )
    prior_copy.start()
    own = slot_of(c)
    kvb[own, 0] = k_ref[...]
    kvb[own, 1] = v_ref[...]
    kvb[own, 2] = pk_ref[...]
    kvb[own, 3] = pv_ref[...]

    barrier = pltpu.get_barrier_semaphore()

    def greet_ctx(i, carry):
        pl.semaphore_signal(
            barrier, inc=1, device_id=(lax.rem(c + i, CTX), t), device_id_type=MESH
        )
        return carry

    def greet_tp(i, carry):
        pl.semaphore_signal(
            barrier, inc=1, device_id=(c, lax.rem(t + i, TP)), device_id_type=MESH
        )
        return carry

    lax.fori_loop(1, CTX, greet_ctx, 0)
    lax.fori_loop(1, TP, greet_tp, 0)
    pl.semaphore_wait(barrier, CTX - 1 + TP - 1)

    def first(half):
        return 0 if half == 0 else 1

    def piece(slot, half, quarter):
        if quarter is None:
            return kvb.at[slot, pl.ds(2 * half, 2)]
        return kvb.at[slot, 2 * half + quarter]

    def kv_copy(chunk, half, quarter, send, dest):
        slot = slot_of(chunk)
        ref = piece(slot, half, quarter)
        recv = kv_recv.at[slot, half, 0 if quarter is None else quarter]
        return remote(ref, ref, send, recv, (dest, t))

    def base(p):
        return c if p == 0 else mate

    def send_desc(kind, p, r, half, way):
        dim1, dim2 = first(half), 1 - first(half)
        step = 1 - 2 * way
        if kind == "p1a":
            return kv_copy(
                base(p), half, None, kv_send.at[p, 0, half, way], neighbour(c, dim1, step)
            )
        if kind == "p1b":
            chunk = neighbour(base(p), dim1, -step)
            return kv_copy(
                chunk, half, way, kv_send.at[p, 1, half, way], neighbour(c, dim1, step)
            )
        row = neighbour(base(p), dim1, r)
        if kind == "p2a":
            return kv_copy(
                row, half, None, kv_send.at[p, 2 + r, half, way], neighbour(c, dim2, step)
            )
        chunk = neighbour(row, dim2, -step)
        return kv_copy(
            chunk, half, way, kv_send.at[p, 6 + r, half, way], neighbour(c, dim2, step)
        )

    def wait_whole(chunk, half):
        kv_copy(chunk, half, None, kv_send.at[0, 0, 0, 0], c).wait_recv()

    def wait_split(chunk, half):
        for quarter in range(2):
            kv_copy(chunk, half, quarter, kv_send.at[0, 0, 0, 0], c).wait_recv()

    def each(fn):
        for half in range(2):
            for way in range(2):
                fn(half, way)

    def row_sends(p, r):
        each(lambda half, way: send_desc("p2a", p, r, half, way).start())

    def own_sends(p):
        each(lambda half, way: send_desc("p1a", p, 0, half, way).start())

    def own_forwards(p):
        def got_one(half, way):
            wait_whole(neighbour(base(p), first(half), 2 * way - 1), half)
            send_desc("p1b", p, 0, half, way).start()

        each(got_one)

    def far_row(p):
        for half in range(2):
            wait_split(neighbour(base(p), first(half), 2), half)
        row_sends(p, 2)

    def forward(p, r):
        def got_one(half, way):
            row = neighbour(base(p), first(half), r)
            wait_whole(neighbour(row, 1 - first(half), 2 * way - 1), half)
            send_desc("p2b", p, r, half, way).start()

        each(got_one)

    def forwards(p):
        def one(r, carry):
            forward(p, r)
            return carry

        lax.fori_loop(0, 4, one, 0)

    def stage_f(p):
        def one(r, carry):
            for half in range(2):
                row = neighbour(base(p), first(half), r)
                wait_split(neighbour(row, 1 - first(half), 2), half)
            return carry

        lax.fori_loop(0, 4, one, 0)

    y_copy = remote(kvb.at[own], kvb.at[own], y_send, y_recv, (mate, t))
    y_got = remote(kvb.at[slot_of(mate)], kvb.at[slot_of(mate)], y_send, y_recv, (mate, t))

    following = lax.rem(c + 1, CTX)
    edge_copies = [
        remote(x_ref.at[pl.ds(ROWS - 16, 16)], edge_x, edge_send.at[0], edge_recv.at[0], (following, t)),
        remote(bc_ref.at[pl.ds(ROWS - 16, 16)], edge_bc, edge_send.at[1], edge_recv.at[1], (following, t)),
    ]
    for copy in edge_copies:
        copy.start()
    y_copy.start()
    own_sends(0)
    row_sends(0, 0)

    row_i = lax.broadcasted_iota(jnp.int32, (ROWS, ROWS), 0)
    col_i = lax.broadcasted_iota(jnp.int32, (ROWS, ROWS), 1)
    lower = row_i >= col_i
    ones_low = jnp.where(lower, 1.0, 0.0).astype(F32)
    ld = ld_ref[...]
    cum = exact_dot(ones_low, ld, NT)
    cum_t[...] = exact_dot(ld, ones_low, NT)
    dt = exact_dot(jnp.where(row_i == col_i, 1.0, 0.0).astype(F32), dt_ref[...], NT)
    aux[:, 0:32] = cum
    aux[:, 32:64] = dt
    aux[:, 64:96] = jnp.exp(cum[ROWS - 1 : ROWS] - cum) * dt
    aux[:, 96:128] = jnp.exp(cum)

    for copy in edge_copies:
        copy.wait_recv()

    at_start = c == 0

    def conv(buffer, edge, own_prior, here, taps):
        buffer[5:8, :] = jnp.where(at_start, own_prior, edge.astype(F32)[13:16])
        buffer[8 : 8 + ROWS, :] = here.astype(F32)
        total = taps[0:1] * buffer[5 : 5 + ROWS, :]
        for k in range(1, 4):
            total = total + taps[k : k + 1] * buffer[5 + k : 5 + k + ROWS, :]
        return silu(total)

    flat_prior = prior_bc[...].astype(F32)
    flat_prior = jnp.concatenate([flat_prior[:, 0], flat_prior[:, 1]], axis=1)
    flat_taps = jnp.concatenate([taps_bc[:, 0], taps_bc[:, 1]], axis=1)
    proj = conv(ext_bc, edge_bc[...], flat_prior, bc_ref[...], flat_taps)
    b_ref[...] = proj[:, :NSTATE].astype(BF16)
    c_ref[...] = proj[:, NSTATE:].astype(BF16)
    g_ref[...] = dot(c_ref[...], b_ref[...], NT)

    left_half = lax.broadcasted_iota(jnp.int32, (ROWS, 128), 1) < 64

    def columns(pair):
        return pl.ds(pl.multiple_of(pair * 128, 128), 128)

    def rolled(pair):
        return pltpu.roll(aux[...], 128 - 2 * pair, 1)

    def spread(lanes, at):
        return jnp.where(left_half, lanes[:, at : at + 1], lanes[:, at + 1 : at + 2])

    def state_copy(h):
        return remote(msg.at[h], got.at[c], st_send.at[h], st_recv.at[c], (h, t))

    def local_states(pair, carry):
        cols = columns(pair)
        act = conv(
            ext, edge_x[:, cols], prior_x[:, cols].astype(F32), x_ref[:, cols], taps_x[:, cols]
        )
        xa[:, cols] = act
        lanes = rolled(pair)
        weighted = (act * spread(lanes, 64)).astype(BF16)
        made = dot(weighted, b_ref[...], TN).astype(BF16)
        row = lax.broadcasted_iota(jnp.int32, (16, NSTATE), 0)
        for sub in range(2):
            h = 2 * pair + sub
            msg[h, 0:64, :] = made[64 * sub : 64 * sub + 64]
            total = jnp.broadcast_to(lanes[ROWS - 1 : ROWS, sub : sub + 1], (16, NSTATE))
            hi = total.astype(BF16).astype(F32)
            mid = (total - hi).astype(BF16).astype(F32)
            low = total - hi - mid
            parts = jnp.where(row == 0, hi, jnp.where(row == 1, mid, jnp.where(row == 2, low, 0.0)))
            msg[h, 64:80, :] = parts.astype(BF16)

            @pl.when(h != c)
            def _():
                state_copy(h).start()

            @pl.when(h == c)
            def _():
                got[c] = msg[h]

        @pl.when(pair == 2)
        def _():
            own_forwards(0)

        @pl.when(pair == 5)
        def _():
            y_got.wait_recv()
            own_sends(1)
            row_sends(0, 1)
            row_sends(0, 3)

        @pl.when(pair == 10)
        def _():
            own_forwards(1)
            far_row(0)
            row_sends(1, 0)

        @pl.when(pair == 15)
        def _():
            row_sends(1, 1)
            row_sends(1, 3)

        return carry

    lax.fori_loop(0, PAIRS, local_states, 0)
    far_row(1)

    acc[...] = jnp.zeros_like(acc)
    top[...] = jnp.full(top.shape, -1e30, F32)

    lane = lax.broadcasted_iota(jnp.int32, (1, GROUP), 1)
    order = 2 * lax.rem(lax.div(lane, ROWS), 4) + lax.div(lane, 4 * ROWS)
    place = lax.rem(c, 8)
    offset = jnp.where(order < place, ROWS, jnp.where(order == place, 0, -ROWS))
    edge_lane = lax.rem(lane, ROWS) - offset
    row_one = lax.broadcasted_iota(jnp.int32, (ROWS, 1), 0)

    def group(x_at, part, heads_of, masked):
        keys = kvb[pl.ds(x_at * 8, 8), part].reshape(GROUP, HD)
        vals = kvb[pl.ds(x_at * 8, 8), part + 1].reshape(GROUP, HD)
        wide = jnp.concatenate([vals, jnp.ones_like(vals)], axis=1)

        def attend(h):
            query = q_ref[:, pl.ds(pl.multiple_of(h * HD, HD), HD)]
            scores = dot(query, keys, NT)
            if masked:
                scores = jnp.where(edge_lane <= row_one, scores, -1e30)
            return scores

        def absorb(h, scores):
            before = top[h]
            new = jnp.maximum(before, jnp.max(scores, axis=1, keepdims=True))
            top[h] = new
            shrink = jnp.exp2((before - new) * COEF)
            weights = jnp.exp2((scores - new[:, 0:1]) * COEF).astype(BF16)
            acc[h] = acc[h] * jnp.concatenate([shrink, shrink], axis=1) + dot(weights, wide)

        ahead = attend(heads_of[0])
        for i, h in enumerate(heads_of):
            scores = ahead
            if i + 1 < len(heads_of):
                ahead = attend(heads_of[i + 1])
            absorb(h, scores)

    def cached(g, carry):
        @pl.when(g == 1)
        def _():
            forwards(0)
            forwards(1)

        @pl.when(g == 3)
        def _():
            stage_f(0)
            stage_f(1)

        far = jnp.where(g == 2, 3, jnp.where(g == 3, 2, g))
        group(lax.rem(lax.div(c, 8) + far, 4), 2, list(range(HEADS)), False)
        return carry

    lax.fori_loop(0, 4, cached, 0)

    prior_copy.wait()

    def back_copy(j):
        here = pl.ds(pl.multiple_of(c * 64, 64), 64)
        return remote(back.at[j], incoming.at[here], in_send.at[j], in_recv.at[c], (j, t))

    def scan(j, carry):
        @pl.when(j != c)
        def _():
            remote(msg.at[j], got.at[j], st_send.at[j], st_recv.at[j], (j, t)).wait_recv()

        now = state[...]
        back[j] = now.astype(BF16)

        @pl.when(j != c)
        def _():
            back_copy(j).start()

        @pl.when(j == c)
        def _():
            incoming[pl.ds(pl.multiple_of(c * 64, 64), 64), :] = now.astype(BF16)

        tail = got[j, 64:80, :].astype(F32)
        total = tail[0:1] + tail[1:2] + tail[2:3]
        state[...] = jnp.exp(total) * now + got[j, 0:64, :].astype(F32)
        return carry

    lax.fori_loop(0, CTX, scan, 0)

    def head_copy(h, i):
        cols = pl.ds(pl.multiple_of((t * HEADS + h) * HD, HD), HD)
        return remote(
            heads.at[:, cols],
            heads.at[:, cols],
            hd_send.at[h, i],
            hd_recv.at[t, h],
            (c, lax.rem(t + i, TP)),
        )

    def block_keys(part, carry):
        heads_of = [part * 4 + i for i in range(4)]

        def earlier(x_at, carry2):
            group(x_at, 0, heads_of, False)
            return carry2

        lax.fori_loop(0, lax.div(c, 8), earlier, 0)
        group(lax.div(c, 8), 0, heads_of, True)
        for h in heads_of:
            full = acc[h]
            cols = pl.ds(pl.multiple_of((t * HEADS + h) * HD, HD), HD)
            heads[:, cols] = (full[:, :HD] / full[:, HD:]).astype(BF16)
            for i in range(1, TP):
                head_copy(h, i).start()
        return carry

    lax.fori_loop(0, 2, block_keys, 0)

    def within_block(pair, carry):
        cols = columns(pair)
        lanes = rolled(pair)
        act = xa[:, cols]
        scaled = (act * spread(lanes, 32)).astype(BF16)
        skips = jnp.where(left_half, skip_ref[2 * pair], skip_ref[2 * pair + 1])
        parts = []
        for sub in range(2):
            h = 2 * pair + sub
            diff = lanes[:, sub : sub + 1] - cum_t[pl.ds(h, 1), :]
            decay = jnp.exp(jnp.where(lower, diff, -1e30))
            parts.append(dot((g_ref[...] * decay).astype(BF16), scaled))
        xa[:, cols] = jnp.where(left_half, parts[0], parts[1]) + skips * act

        return carry

    lax.fori_loop(0, PAIRS, within_block, 0)

    def in_wait(j, carry):
        @pl.when(j != c)
        def _():
            rows = pl.ds(pl.multiple_of(j * 64, 64), 64)
            remote(back.at[j], incoming.at[rows], in_send.at[j], in_recv.at[j], (j, t)).wait_recv()

        return carry

    lax.fori_loop(0, CTX, in_wait, 0)
    squares[...] = jnp.zeros_like(squares)

    def mix(pair, carry):
        cols = columns(pair)
        lanes = rolled(pair)
        earlier = dot(c_ref[...], incoming[cols, :], NT)
        mixed = xa[:, cols] + spread(lanes, 96) * earlier
        gated = mixed * silu(z_ref[:, cols].astype(F32))
        squares[...] += gated * gated
        xa[:, cols] = gated
        return carry

    lax.fori_loop(0, PAIRS, mix, 0)
    mean = jnp.sum(squares[...], axis=1, keepdims=True) * (1.0 / WIDE)
    squares[...] = jnp.broadcast_to(lax.rsqrt(mean + 1e-05), squares.shape)

    def norm(pair, carry):
        cols = columns(pair)
        ssm_ref[:, cols] = (xa[:, cols] * squares[...] * gain_ref[:, cols]).astype(BF16)
        return carry

    lax.fori_loop(0, PAIRS, norm, 0)

    def head_wait(h, carry):
        for i in range(1, TP):
            src = lax.rem(t + i, TP)
            cols = pl.ds(pl.multiple_of((src * HEADS + h) * HD, HD), HD)
            remote(
                heads.at[:, cols], heads.at[:, cols], hd_send.at[h, i], hd_recv.at[src, h], (c, src)
            ).wait_recv()
        return carry

    lax.fori_loop(0, HEADS, head_wait, 0)
    w_copy.wait()

    def project(n, carry):
        cols = pl.ds(pl.multiple_of(n * 256, 256), 256)
        attn_ref[:, cols] = dot(heads[...], w_ref[:, cols]).astype(BF16)
        return carry

    lax.fori_loop(0, WIDE // 256, project, 0)

    for copy in edge_copies:
        copy.wait_send()
    y_copy.wait_send()
    for p in range(2):
        each(lambda half, way: send_desc("p1a", p, 0, half, way).wait_send())
        each(lambda half, way: send_desc("p1b", p, 0, half, way).wait_send())

        def sent(r, carry):
            each(lambda half, way: send_desc("p2a", p, r, half, way).wait_send())
            each(lambda half, way: send_desc("p2b", p, r, half, way).wait_send())
            return carry

        lax.fori_loop(0, 4, sent, 0)

    def states_sent(j, carry):
        @pl.when(j != c)
        def _():
            state_copy(j).wait_send()
            back_copy(j).wait_send()

        return carry

    lax.fori_loop(0, CTX, states_sent, 0)

    def heads_sent(h, carry):
        for i in range(1, TP):
            head_copy(h, i).wait_send()
        return carry

    lax.fori_loop(0, HEADS, heads_sent, 0)


def per_device(
    queries,
    keys,
    values,
    prior_keys,
    prior_values,
    out_weight,
    ssm_x,
    ssm_bc,
    gate_z,
    conv_x,
    conv_bc,
    conv_prior_x,
    conv_prior_bc,
    step_dt,
    log_decay,
    skip_d,
    ssm_prior,
    norm_gain,
):
    vm = pl.BlockSpec(memory_space=pltpu.VMEM)
    anywhere = pl.BlockSpec(memory_space=pl.ANY)
    small = pl.BlockSpec(memory_space=pltpu.SMEM)
    return pl.pallas_call(
        kernel,
        out_shape=(
            jax.ShapeDtypeStruct((ROWS, WIDE), BF16),
            jax.ShapeDtypeStruct((ROWS, WIDE), BF16),
        ),
        in_specs=[vm] * 5 + [anywhere] + [vm] * 9 + [small, anywhere, vm],
        out_specs=(vm, vm),
        scratch_shapes=[
            pltpu.VMEM((CTX, 4, ROWS, HD), BF16),
            pltpu.VMEM((HEADS, ROWS, 2 * HD), F32),
            pltpu.VMEM((HEADS, ROWS, HD), F32),
            pltpu.VMEM((ROWS, TP * HEADS * HD), BF16),
            pltpu.VMEM((TP * HEADS * HD, WIDE), BF16),
            pltpu.VMEM((16, WIDE), BF16),
            pltpu.VMEM((16, 2 * NSTATE), BF16),
            pltpu.VMEM((ROWS + 8, 128), F32),
            pltpu.VMEM((ROWS + 8, 2 * NSTATE), F32),
            pltpu.VMEM((ROWS, NSTATE), BF16),
            pltpu.VMEM((ROWS, NSTATE), BF16),
            pltpu.VMEM((ROWS, ROWS), F32),
            pltpu.VMEM((ROWS, 128), F32),
            pltpu.VMEM((SH, ROWS), F32),
            pltpu.VMEM((ROWS, WIDE), F32),
            pltpu.VMEM((SH, MSG, NSTATE), BF16),
            pltpu.VMEM((CTX, MSG, NSTATE), BF16),
            pltpu.VMEM((64, NSTATE), F32),
            pltpu.VMEM((CTX, 64, NSTATE), BF16),
            pltpu.VMEM((WIDE, NSTATE), BF16),
            pltpu.VMEM((ROWS, 128), F32),
            pltpu.SemaphoreType.DMA,
            pltpu.SemaphoreType.DMA,
            pltpu.SemaphoreType.DMA,
            pltpu.SemaphoreType.DMA,
            pltpu.SemaphoreType.DMA((2, 10, 2, 2)),
            pltpu.SemaphoreType.DMA((CTX, 2, 2)),
            pltpu.SemaphoreType.DMA((2,)),
            pltpu.SemaphoreType.DMA((2,)),
            pltpu.SemaphoreType.DMA((CTX,)),
            pltpu.SemaphoreType.DMA((CTX,)),
            pltpu.SemaphoreType.DMA((CTX,)),
            pltpu.SemaphoreType.DMA((CTX,)),
            pltpu.SemaphoreType.DMA((HEADS, TP)),
            pltpu.SemaphoreType.DMA((TP, HEADS)),
        ],
        compiler_params=pltpu.CompilerParams(
            collective_id=0, has_side_effects=True, vmem_limit_bytes=60 * 2**20
        ),
        name="hybrid",
    )(
        queries,
        keys,
        values,
        prior_keys,
        prior_values,
        out_weight,
        ssm_x,
        ssm_bc.reshape(ROWS, 2 * NSTATE),
        gate_z,
        conv_x,
        conv_bc,
        conv_prior_x,
        conv_prior_bc,
        step_dt.T,
        log_decay.T,
        skip_d,
        ssm_prior.reshape(WIDE, NSTATE),
        norm_gain.reshape(1, WIDE),
    )


def solution(mesh):
    in_specs = (
        P("ctx", "tp"),
        P("ctx", "tp"),
        P("ctx", "tp"),
        P("ctx", "tp"),
        P("ctx", "tp"),
        P(None, "tp"),
        P("ctx", "tp"),
        P("ctx", None, "tp"),
        P("ctx", "tp"),
        P(None, "tp"),
        P(None, None, "tp"),
        P(None, "tp"),
        P(None, None, "tp"),
        P("ctx", "tp"),
        P("ctx", "tp"),
        P("tp"),
        P("tp", None, None),
        P("tp"),
    )
    out_specs = (P("ctx", "tp"), P("ctx", "tp"))
    return jax.shard_map(
        per_device, mesh=mesh, in_specs=in_specs, out_specs=out_specs, check_vma=False
    )
```

```python
import functools

import jax
import jax.numpy as jnp
from jax import lax
from jax.experimental import pallas as pl
from jax.experimental.pallas import tpu as pltpu
from jax.sharding import PartitionSpec as P

MESH = pl.DeviceIdType.MESH
F32 = jnp.float32
BF16 = jnp.bfloat16
HD = 128
CTX = 32
TP = 4
ROWS = 256
HEADS = 8
SH = 32
WIDE = 2048
PAIRS = 16
NSTATE = 256
MSG = 80
GROUP = 8 * ROWS
COEF = 1.4426950408889634 / (HD**0.5)
NT = (((1,), (1,)), ((), ()))
TN = (((0,), (0,)), ((), ()))


def dot(a, b, dims=(((1,), (0,)), ((), ()))):
    return lax.dot_general(a, b, dims, preferred_element_type=F32)


def exact_dot(a, b, dims):
    return lax.dot_general(
        a, b, dims, preferred_element_type=F32, precision=lax.Precision.HIGHEST
    )


def silu(v):
    return v / (1.0 + jnp.exp(-v))


def neighbour(c, dim, step):
    if dim == 0:
        return lax.rem(c + 8 * step + 32, 32)
    z = lax.rem(lax.div(c, 2), 4)
    return c + 2 * (lax.rem(z + step + 4, 4) - z)


def slot_of(c, half):
    x, z, y = lax.div(c, 8), lax.rem(lax.div(c, 2), 4), lax.rem(c, 2)
    return z * 8 + y * 4 + x if half == 0 else x * 8 + y * 4 + z


def kernel(
    q_ref,
    k_ref,
    v_ref,
    pk_ref,
    pv_ref,
    w_hbm,
    x_ref,
    bc_ref,
    z_ref,
    taps_x,
    taps_bc,
    prior_x,
    prior_bc,
    dt_ref,
    ld_ref,
    skip_ref,
    prior_hbm,
    gain_ref,
    attn_ref,
    ssm_ref,
    kvb,
    acc,
    top,
    heads,
    w_ref,
    edge_x,
    edge_bc,
    ext,
    ext_bc,
    b_ref,
    c_ref,
    g_ref,
    aux,
    cum_t,
    xa,
    msg,
    got,
    state,
    back,
    incoming,
    squares,
    w_sem,
    prior_sem,
    y_send,
    y_recv,
    kv_send,
    kv_recv,
    edge_send,
    edge_recv,
    st_send,
    st_recv,
    in_send,
    in_recv,
    hd_send,
    hd_recv,
):
    c = lax.axis_index("ctx")
    t = lax.axis_index("tp")
    mate = c + 1 - 2 * lax.rem(c, 2)

    def remote(src, dst, send, recv, dev):
        return pltpu.make_async_remote_copy(
            src_ref=src,
            dst_ref=dst,
            send_sem=send,
            recv_sem=recv,
            device_id=dev,
            device_id_type=MESH,
        )

    w_copy = pltpu.make_async_copy(w_hbm, w_ref, w_sem)
    w_copy.start()
    prior_copy = pltpu.make_async_copy(
        prior_hbm.at[pl.ds(pl.multiple_of(c * 64, 64), 64)], state, prior_sem
    )
    prior_copy.start()
    barrier = pltpu.get_barrier_semaphore()

    def greet_ctx(i, carry):
        pl.semaphore_signal(
            barrier, inc=1, device_id=(lax.rem(c + i, CTX), t), device_id_type=MESH
        )
        return carry

    def greet_tp(i, carry):
        pl.semaphore_signal(
            barrier, inc=1, device_id=(c, lax.rem(t + i, TP)), device_id_type=MESH
        )
        return carry

    lax.fori_loop(1, CTX, greet_ctx, 0)
    lax.fori_loop(1, TP, greet_tp, 0)
    kvb[0, slot_of(c, 0), 0] = k_ref[...]
    kvb[0, slot_of(c, 0), 1] = v_ref[...]
    kvb[1, slot_of(c, 1), 0] = pk_ref[...]
    kvb[1, slot_of(c, 1), 1] = pv_ref[...]

    row_i = lax.broadcasted_iota(jnp.int32, (ROWS, ROWS), 0)
    col_i = lax.broadcasted_iota(jnp.int32, (ROWS, ROWS), 1)
    lower = row_i >= col_i
    ones_low = jnp.where(lower, 1.0, 0.0).astype(F32)
    ld = ld_ref[...]
    cum = exact_dot(ones_low, ld, NT)
    cum_t[...] = exact_dot(ld, ones_low, NT)
    dt = exact_dot(jnp.where(row_i == col_i, 1.0, 0.0).astype(F32), dt_ref[...], NT)
    aux[:, 0:32] = cum
    aux[:, 32:64] = dt
    aux[:, 64:96] = jnp.exp(cum[ROWS - 1 : ROWS] - cum) * dt
    aux[:, 96:128] = jnp.exp(cum)

    pl.semaphore_wait(barrier, CTX - 1 + TP - 1)

    def first(half):
        return 0 if half == 0 else 1

    def piece(slot, half, quarter):
        if quarter is None:
            return kvb.at[half, slot]
        return kvb.at[half, slot, quarter]

    def kv_copy(chunk, half, quarter, send, dest):
        slot = slot_of(chunk, half)
        ref = piece(slot, half, quarter)
        recv = kv_recv.at[slot, half, 0 if quarter is None else quarter]
        return remote(ref, ref, send, recv, (dest, t))

    def base(p):
        return c if p == 0 else mate

    def send_desc(kind, p, r, half, way):
        dim1, dim2 = first(half), 1 - first(half)
        step = 1 - 2 * way
        if kind == "p1a":
            return kv_copy(
                base(p), half, None, kv_send.at[p, 0, half, way], neighbour(c, dim1, step)
            )
        if kind == "p1b":
            chunk = neighbour(base(p), dim1, -step)
            return kv_copy(
                chunk, half, way, kv_send.at[p, 1, half, way], neighbour(c, dim1, step)
            )
        row = neighbour(base(p), dim1, r)
        if kind == "p2a":
            return kv_copy(
                row, half, None, kv_send.at[p, 2 + r, half, way], neighbour(c, dim2, step)
            )
        chunk = neighbour(row, dim2, -step)
        return kv_copy(
            chunk, half, way, kv_send.at[p, 6 + r, half, way], neighbour(c, dim2, step)
        )

    def wait_whole(chunk, half):
        kv_copy(chunk, half, None, kv_send.at[0, 0, 0, 0], c).wait_recv()

    def wait_split(chunk, half):
        for quarter in range(2):
            kv_copy(chunk, half, quarter, kv_send.at[0, 0, 0, 0], c).wait_recv()

    def each(fn):
        for half in range(2):
            for way in range(2):
                fn(half, way)

    def row_sends(p, r):
        each(lambda half, way: send_desc("p2a", p, r, half, way).start())

    def own_sends(p):
        each(lambda half, way: send_desc("p1a", p, 0, half, way).start())

    def own_forwards(p):
        def got_one(half, way):
            wait_whole(neighbour(base(p), first(half), 2 * way - 1), half)
            send_desc("p1b", p, 0, half, way).start()

        each(got_one)

    def far_row(p):
        for half in range(2):
            wait_split(neighbour(base(p), first(half), 2), half)
        row_sends(p, 2)

    def forward(p, r):
        def got_one(half, way):
            row = neighbour(base(p), first(half), r)
            wait_whole(neighbour(row, 1 - first(half), 2 * way - 1), half)
            send_desc("p2b", p, r, half, way).start()

        each(got_one)

    def forwards(p):
        def one(r, carry):
            forward(p, r)
            return carry

        lax.fori_loop(0, 4, one, 0)

    def stage_f(p):
        def one(r, carry):
            for half in range(2):
                row = neighbour(base(p), first(half), r)
                wait_split(neighbour(row, 1 - first(half), 2), half)
            return carry

        lax.fori_loop(0, 4, one, 0)

    def y_copy(half, owner):
        ref = kvb.at[half, slot_of(owner, half)]
        return remote(ref, ref, y_send.at[half], y_recv.at[half], (mate, t))

    following = lax.rem(c + 1, CTX)
    edge_copies = [
        remote(x_ref.at[pl.ds(ROWS - 16, 16)], edge_x, edge_send.at[0], edge_recv.at[0], (following, t)),
        remote(bc_ref.at[pl.ds(ROWS - 16, 16)], edge_bc, edge_send.at[1], edge_recv.at[1], (following, t)),
    ]
    for copy in edge_copies:
        copy.start()
    for half in range(2):
        y_copy(half, c).start()
    own_sends(0)
    row_sends(0, 0)

    for copy in edge_copies:
        copy.wait_recv()

    at_start = c == 0

    def conv(buffer, edge, own_prior, here, taps):
        buffer[5:8, :] = jnp.where(at_start, own_prior, edge.astype(F32)[13:16])
        buffer[8 : 8 + ROWS, :] = here.astype(F32)
        total = taps[0:1] * buffer[5 : 5 + ROWS, :]
        for k in range(1, 4):
            total = total + taps[k : k + 1] * buffer[5 + k : 5 + k + ROWS, :]
        return silu(total)

    flat_prior = prior_bc[...].astype(F32)
    flat_prior = jnp.concatenate([flat_prior[:, 0], flat_prior[:, 1]], axis=1)
    flat_taps = jnp.concatenate([taps_bc[:, 0], taps_bc[:, 1]], axis=1)
    proj = conv(ext_bc, edge_bc[...], flat_prior, bc_ref[...], flat_taps)
    b_ref[...] = proj[:, :NSTATE].astype(BF16)
    c_ref[...] = proj[:, NSTATE:].astype(BF16)
    g_ref[...] = dot(c_ref[...], b_ref[...], NT)

    left_half = lax.broadcasted_iota(jnp.int32, (ROWS, 128), 1) < 64

    def columns(pair):
        return pl.ds(pl.multiple_of(pair * 128, 128), 128)

    def rolled(pair):
        return pltpu.roll(aux[...], 128 - 2 * pair, 1)

    def spread(lanes, at):
        return jnp.where(left_half, lanes[:, at : at + 1], lanes[:, at + 1 : at + 2])

    def state_copy(h):
        return remote(msg.at[h], got.at[c], st_send.at[h], st_recv.at[c], (h, t))

    def local_states(pair, carry):
        cols = columns(pair)
        act = conv(
            ext, edge_x[:, cols], prior_x[:, cols].astype(F32), x_ref[:, cols], taps_x[:, cols]
        )
        xa[:, cols] = act
        lanes = rolled(pair)
        weighted = (act * spread(lanes, 64)).astype(BF16)
        made = dot(weighted, b_ref[...], TN).astype(BF16)
        row = lax.broadcasted_iota(jnp.int32, (16, NSTATE), 0)
        for sub in range(2):
            h = 2 * pair + sub
            msg[h, 0:64, :] = made[64 * sub : 64 * sub + 64]
            total = jnp.broadcast_to(lanes[ROWS - 1 : ROWS, sub : sub + 1], (16, NSTATE))
            hi = total.astype(BF16).astype(F32)
            mid = (total - hi).astype(BF16).astype(F32)
            low = total - hi - mid
            parts = jnp.where(row == 0, hi, jnp.where(row == 1, mid, jnp.where(row == 2, low, 0.0)))
            msg[h, 64:80, :] = parts.astype(BF16)

            @pl.when(h != c)
            def _():
                state_copy(h).start()

            @pl.when(h == c)
            def _():
                got[c] = msg[h]

        @pl.when(pair == 2)
        def _():
            own_forwards(0)

        @pl.when(pair == 5)
        def _():
            for half in range(2):
                y_copy(half, mate).wait_recv()
            own_sends(1)
            row_sends(0, 1)
            row_sends(0, 3)

        @pl.when(pair == 10)
        def _():
            own_forwards(1)
            far_row(0)
            row_sends(1, 0)

        @pl.when(pair == 15)
        def _():
            row_sends(1, 1)
            row_sends(1, 3)

        return carry

    lax.fori_loop(0, PAIRS, local_states, 0)
    far_row(1)

    acc[...] = jnp.zeros_like(acc)
    top[...] = jnp.full(top.shape, -1e30, F32)

    lane = lax.broadcasted_iota(jnp.int32, (1, GROUP), 1)
    row_one = lax.broadcasted_iota(jnp.int32, (ROWS, 1), 0)

    def group(half, at, heads_of):
        keys = kvb[half, pl.ds(at * 8, 8), 0].reshape(GROUP, HD)
        vals = kvb[half, pl.ds(at * 8, 8), 1].reshape(GROUP, HD)
        wide = jnp.concatenate([vals, jnp.ones_like(vals)], axis=1)
        if half == 0:
            order = lax.rem(lax.div(lane, ROWS), 4) * 8 + at * 2 + lax.div(lane, 4 * ROWS)
            offset = jnp.where(order < c, ROWS, jnp.where(order == c, 0, -ROWS))
            edge_lane = lax.rem(lane, ROWS) - offset

        def attend(h):
            query = q_ref[:, pl.ds(pl.multiple_of(h * HD, HD), HD)]
            scores = dot(query, keys, NT)
            if half == 0:
                scores = jnp.where(edge_lane <= row_one, scores, -1e30)
            return scores

        def absorb(h, scores):
            before = top[h]
            new = jnp.maximum(before, jnp.max(scores, axis=1, keepdims=True))
            top[h] = new
            shrink = jnp.exp2((before - new) * COEF)
            weights = jnp.exp2((scores - new[:, 0:1]) * COEF).astype(BF16)
            acc[h] = acc[h] * jnp.concatenate([shrink, shrink], axis=1) + dot(weights, wide)

        ahead = attend(heads_of[0])
        for i, h in enumerate(heads_of):
            scores = ahead
            if i + 1 < len(heads_of):
                ahead = attend(heads_of[i + 1])
            absorb(h, scores)

    prior_copy.wait()

    def back_copy(j):
        here = pl.ds(pl.multiple_of(c * 64, 64), 64)
        return remote(back.at[j], incoming.at[here], in_send.at[j], in_recv.at[c], (j, t))

    def scan(j, carry):
        @pl.when(j != c)
        def _():
            remote(msg.at[j], got.at[j], st_send.at[j], st_recv.at[j], (j, t)).wait_recv()

        now = state[...]
        back[j] = now.astype(BF16)

        @pl.when(j != c)
        def _():
            back_copy(j).start()

        @pl.when(j == c)
        def _():
            incoming[pl.ds(pl.multiple_of(c * 64, 64), 64), :] = now.astype(BF16)

        tail = got[j, 64:80, :].astype(F32)
        total = tail[0:1] + tail[1:2] + tail[2:3]
        state[...] = jnp.exp(total) * now + got[j, 0:64, :].astype(F32)
        return carry


    def within_block(pair, carry):
        cols = columns(pair)
        lanes = rolled(pair)
        act = xa[:, cols]
        scaled = (act * spread(lanes, 32)).astype(BF16)
        skips = jnp.where(left_half, skip_ref[2 * pair], skip_ref[2 * pair + 1])
        parts = []
        for sub in range(2):
            h = 2 * pair + sub
            diff = lanes[:, sub : sub + 1] - cum_t[pl.ds(h, 1), :]
            decay = jnp.exp(jnp.where(lower, diff, -1e30))
            parts.append(dot((g_ref[...] * decay).astype(BF16), scaled))
        xa[:, cols] = jnp.where(left_half, parts[0], parts[1]) + skips * act

        return carry


    def at_of(half, far):
        here = lax.div(c, 8) if half == 1 else lax.rem(lax.div(c, 2), 4)
        return lax.rem(here + far, 4)

    def near(g, carry):
        far = jnp.where(g == 2, 3, g)

        @pl.when(g == 1)
        def _():
            lax.fori_loop(0, PAIRS, within_block, 0)
            forwards(1)

        group(1, at_of(1, far), list(range(HEADS)))

        @pl.when(g == 0)
        def _():
            forwards(0)

        group(0, at_of(0, far), list(range(HEADS)))
        return carry

    lax.fori_loop(0, 3, near, 0)
    stage_f(0)
    stage_f(1)
    lax.fori_loop(0, CTX, scan, 0)

    other_core = t + 1 - 2 * lax.rem(t, 2)
    across = lax.rem(t + 2, TP)

    def head_copy(src, h, dest, kind):
        cols = pl.ds(pl.multiple_of((src * HEADS + h) * HD, HD), HD)
        return remote(
            heads.at[:, cols], heads.at[:, cols], hd_send.at[h, kind], hd_recv.at[src, h], (c, dest)
        )

    def pass_on(h, carry):
        head_copy(across, h, across, 0).wait_recv()
        head_copy(across, h, other_core, 2).start()
        return carry

    def last(part, carry):
        heads_of = [part * 4 + i for i in range(4)]
        group(1, at_of(1, 2), heads_of)
        group(0, at_of(0, 2), heads_of)
        for h in heads_of:
            full = acc[h]
            cols = pl.ds(pl.multiple_of((t * HEADS + h) * HD, HD), HD)
            heads[:, cols] = (full[:, :HD] / full[:, HD:]).astype(BF16)
            head_copy(t, h, across, 0).start()
            head_copy(t, h, other_core, 1).start()
        return carry

    lax.fori_loop(0, 2, last, 0)
    lax.fori_loop(0, 4, pass_on, 0)

    def in_wait(j, carry):
        @pl.when(j != c)
        def _():
            rows = pl.ds(pl.multiple_of(j * 64, 64), 64)
            remote(back.at[j], incoming.at[rows], in_send.at[j], in_recv.at[j], (j, t)).wait_recv()

        return carry

    lax.fori_loop(0, CTX, in_wait, 0)
    squares[...] = jnp.zeros_like(squares)

    def mix(pair, carry):
        cols = columns(pair)
        lanes = rolled(pair)
        earlier = dot(c_ref[...], incoming[cols, :], NT)
        mixed = xa[:, cols] + spread(lanes, 96) * earlier
        gated = mixed * silu(z_ref[:, cols].astype(F32))
        squares[...] += gated * gated
        xa[:, cols] = gated
        return carry

    lax.fori_loop(0, PAIRS, mix, 0)
    mean = jnp.sum(squares[...], axis=1, keepdims=True) * (1.0 / WIDE)
    squares[...] = jnp.broadcast_to(lax.rsqrt(mean + 1e-05), squares.shape)

    def norm(pair, carry):
        cols = columns(pair)
        ssm_ref[:, cols] = (xa[:, cols] * squares[...] * gain_ref[:, cols]).astype(BF16)
        return carry

    lax.fori_loop(0, PAIRS, norm, 0)

    lax.fori_loop(4, HEADS, pass_on, 0)

    def head_wait(h, carry):
        head_copy(other_core, h, other_core, 1).wait_recv()
        head_copy(lax.rem(other_core + 2, TP), h, other_core, 2).wait_recv()
        return carry

    lax.fori_loop(0, HEADS, head_wait, 0)
    w_copy.wait()

    def project(n, carry):
        cols = pl.ds(pl.multiple_of(n * 256, 256), 256)
        attn_ref[:, cols] = dot(heads[...], w_ref[:, cols]).astype(BF16)
        return carry

    lax.fori_loop(0, WIDE // 256, project, 0)

    for copy in edge_copies:
        copy.wait_send()
    for half in range(2):
        y_copy(half, c).wait_send()
    for p in range(2):
        each(lambda half, way: send_desc("p1a", p, 0, half, way).wait_send())
        each(lambda half, way: send_desc("p1b", p, 0, half, way).wait_send())

        def sent(r, carry):
            each(lambda half, way: send_desc("p2a", p, r, half, way).wait_send())
            each(lambda half, way: send_desc("p2b", p, r, half, way).wait_send())
            return carry

        lax.fori_loop(0, 4, sent, 0)

    def states_sent(j, carry):
        @pl.when(j != c)
        def _():
            state_copy(j).wait_send()
            back_copy(j).wait_send()

        return carry

    lax.fori_loop(0, CTX, states_sent, 0)

    def heads_sent(h, carry):
        head_copy(t, h, across, 0).wait_send()
        head_copy(t, h, other_core, 1).wait_send()
        head_copy(across, h, other_core, 2).wait_send()
        return carry

    lax.fori_loop(0, HEADS, heads_sent, 0)


def per_device(
    queries,
    keys,
    values,
    prior_keys,
    prior_values,
    out_weight,
    ssm_x,
    ssm_bc,
    gate_z,
    conv_x,
    conv_bc,
    conv_prior_x,
    conv_prior_bc,
    step_dt,
    log_decay,
    skip_d,
    ssm_prior,
    norm_gain,
):
    vm = pl.BlockSpec(memory_space=pltpu.VMEM)
    anywhere = pl.BlockSpec(memory_space=pl.ANY)
    small = pl.BlockSpec(memory_space=pltpu.SMEM)
    return pl.pallas_call(
        kernel,
        out_shape=(
            jax.ShapeDtypeStruct((ROWS, WIDE), BF16),
            jax.ShapeDtypeStruct((ROWS, WIDE), BF16),
        ),
        in_specs=[vm] * 5 + [anywhere] + [vm] * 9 + [small, anywhere, vm],
        out_specs=(vm, vm),
        scratch_shapes=[
            pltpu.VMEM((2, CTX, 2, ROWS, HD), BF16),
            pltpu.VMEM((HEADS, ROWS, 2 * HD), F32),
            pltpu.VMEM((HEADS, ROWS, HD), F32),
            pltpu.VMEM((ROWS, TP * HEADS * HD), BF16),
            pltpu.VMEM((TP * HEADS * HD, WIDE), BF16),
            pltpu.VMEM((16, WIDE), BF16),
            pltpu.VMEM((16, 2 * NSTATE), BF16),
            pltpu.VMEM((ROWS + 8, 128), F32),
            pltpu.VMEM((ROWS + 8, 2 * NSTATE), F32),
            pltpu.VMEM((ROWS, NSTATE), BF16),
            pltpu.VMEM((ROWS, NSTATE), BF16),
            pltpu.VMEM((ROWS, ROWS), F32),
            pltpu.VMEM((ROWS, 128), F32),
            pltpu.VMEM((SH, ROWS), F32),
            pltpu.VMEM((ROWS, WIDE), F32),
            pltpu.VMEM((SH, MSG, NSTATE), BF16),
            pltpu.VMEM((CTX, MSG, NSTATE), BF16),
            pltpu.VMEM((64, NSTATE), F32),
            pltpu.VMEM((CTX, 64, NSTATE), BF16),
            pltpu.VMEM((WIDE, NSTATE), BF16),
            pltpu.VMEM((ROWS, 128), F32),
            pltpu.SemaphoreType.DMA,
            pltpu.SemaphoreType.DMA,
            pltpu.SemaphoreType.DMA((2,)),
            pltpu.SemaphoreType.DMA((2,)),
            pltpu.SemaphoreType.DMA((2, 10, 2, 2)),
            pltpu.SemaphoreType.DMA((CTX, 2, 2)),
            pltpu.SemaphoreType.DMA((2,)),
            pltpu.SemaphoreType.DMA((2,)),
            pltpu.SemaphoreType.DMA((CTX,)),
            pltpu.SemaphoreType.DMA((CTX,)),
            pltpu.SemaphoreType.DMA((CTX,)),
            pltpu.SemaphoreType.DMA((CTX,)),
            pltpu.SemaphoreType.DMA((HEADS, 3)),
            pltpu.SemaphoreType.DMA((TP, HEADS)),
        ],
        compiler_params=pltpu.CompilerParams(
            collective_id=0, has_side_effects=True, vmem_limit_bytes=60 * 2**20
        ),
        name="hybrid",
    )(
        queries,
        keys,
        values,
        prior_keys,
        prior_values,
        out_weight,
        ssm_x,
        ssm_bc.reshape(ROWS, 2 * NSTATE),
        gate_z,
        conv_x,
        conv_bc,
        conv_prior_x,
        conv_prior_bc,
        step_dt.T,
        log_decay.T,
        skip_d,
        ssm_prior.reshape(WIDE, NSTATE),
        norm_gain.reshape(1, WIDE),
    )


def solution(mesh):
    in_specs = (
        P("ctx", "tp"),
        P("ctx", "tp"),
        P("ctx", "tp"),
        P("ctx", "tp"),
        P("ctx", "tp"),
        P(None, "tp"),
        P("ctx", "tp"),
        P("ctx", None, "tp"),
        P("ctx", "tp"),
        P(None, "tp"),
        P(None, None, "tp"),
        P(None, "tp"),
        P(None, None, "tp"),
        P("ctx", "tp"),
        P("ctx", "tp"),
        P("tp"),
        P("tp", None, None),
        P("tp"),
    )
    out_specs = (P("ctx", "tp"), P("ctx", "tp"))
    return jax.shard_map(
        per_device, mesh=mesh, in_specs=in_specs, out_specs=out_specs, check_vma=False
    )
```

```python
import functools

import jax
import jax.numpy as jnp
from jax import lax
from jax.experimental import pallas as pl
from jax.experimental.pallas import tpu as pltpu
from jax.sharding import PartitionSpec as P

MESH = pl.DeviceIdType.MESH
F32 = jnp.float32
BF16 = jnp.bfloat16
HD = 128
CTX = 32
TP = 4
ROWS = 256
HEADS = 8
SH = 32
WIDE = 2048
PAIRS = 16
NSTATE = 256
MSG = 80
GROUP = 8 * ROWS
SPOTS = CTX // 2
COEF = 1.4426950408889634 / (HD**0.5)
NT = (((1,), (1,)), ((), ()))
TN = (((0,), (0,)), ((), ()))


def dot(a, b, dims=(((1,), (0,)), ((), ()))):
    return lax.dot_general(a, b, dims, preferred_element_type=F32)


def exact_dot(a, b, dims):
    return lax.dot_general(
        a, b, dims, preferred_element_type=F32, precision=lax.Precision.HIGHEST
    )


def silu(v):
    return v / (1.0 + jnp.exp(-v))


def neighbour(c, dim, step):
    if dim == 0:
        return lax.rem(c + 8 * step + 32, 32)
    z = lax.rem(lax.div(c, 2), 4)
    return c + 2 * (lax.rem(z + step + 4, 4) - z)


def slot_of(c, half):
    x, z, y = lax.div(c, 8), lax.rem(lax.div(c, 2), 4), lax.rem(c, 2)
    return z * 8 + y * 4 + x if half == 0 else x * 8 + y * 4 + z


def kernel(
    q_ref,
    k_ref,
    v_ref,
    pk_ref,
    pv_ref,
    w_hbm,
    x_ref,
    bc_ref,
    z_ref,
    taps_x,
    taps_bc,
    prior_x,
    prior_bc,
    dt_ref,
    ld_ref,
    skip_ref,
    prior_hbm,
    gain_ref,
    attn_ref,
    ssm_ref,
    kvb,
    acc,
    top,
    heads,
    w_ref,
    edge_x,
    edge_bc,
    ext,
    ext_bc,
    b_ref,
    c_ref,
    g_ref,
    aux,
    cum_t,
    xa,
    msg,
    from_mate,
    comb,
    got,
    state,
    back,
    inc_pair,
    out_mate,
    incoming,
    squares,
    w_sem,
    prior_sem,
    y_send,
    y_recv,
    kv_send,
    kv_recv,
    edge_send,
    edge_recv,
    mate_send,
    mate_recv,
    st_send,
    st_recv,
    in_send,
    in_recv,
    out_send,
    out_recv,
    hd_send,
    hd_recv,
):
    c = lax.axis_index("ctx")
    t = lax.axis_index("tp")
    side = lax.rem(c, 2)
    spot = lax.div(c, 2)
    mate = c + 1 - 2 * side
    mine = SPOTS * side
    theirs = SPOTS * (1 - side)

    def remote(src, dst, send, recv, dev):
        return pltpu.make_async_remote_copy(
            src_ref=src,
            dst_ref=dst,
            send_sem=send,
            recv_sem=recv,
            device_id=dev,
            device_id_type=MESH,
        )

    w_copy = pltpu.make_async_copy(w_hbm, w_ref, w_sem)
    w_copy.start()
    prior_copy = pltpu.make_async_copy(
        prior_hbm.at[pl.ds(pl.multiple_of((mine + spot) * 64, 64), 64)], state, prior_sem
    )
    prior_copy.start()
    barrier = pltpu.get_barrier_semaphore()

    def greet(dev):
        pl.semaphore_signal(barrier, inc=1, device_id=dev, device_id_type=MESH)

    def greet_ctx(i, carry):
        greet((2 * lax.rem(spot + i, SPOTS) + side, t))
        return carry

    lax.fori_loop(1, SPOTS, greet_ctx, 0)
    greet((mate, t))
    greet((lax.rem(c + 2 * side - 1 + CTX, CTX), t))
    greet((c, t + 1 - 2 * lax.rem(t, 2)))
    greet((c, lax.rem(t + 2, TP)))
    kvb[0, slot_of(c, 0), 0] = k_ref[...]
    kvb[0, slot_of(c, 0), 1] = v_ref[...]
    kvb[1, slot_of(c, 1), 0] = pk_ref[...]
    kvb[1, slot_of(c, 1), 1] = pv_ref[...]

    row_i = lax.broadcasted_iota(jnp.int32, (ROWS, ROWS), 0)
    col_i = lax.broadcasted_iota(jnp.int32, (ROWS, ROWS), 1)
    lower = row_i >= col_i
    ones_low = jnp.where(lower, 1.0, 0.0).astype(F32)
    ld = ld_ref[...]
    cum = exact_dot(ones_low, ld, NT)
    cum_t[...] = exact_dot(ld, ones_low, NT)
    dt = exact_dot(jnp.where(row_i == col_i, 1.0, 0.0).astype(F32), dt_ref[...], NT)
    aux[:, 0:32] = cum
    aux[:, 32:64] = dt
    aux[:, 64:96] = jnp.exp(cum[ROWS - 1 : ROWS] - cum) * dt
    aux[:, 96:128] = jnp.exp(cum)

    pl.semaphore_wait(barrier, SPOTS + 3)

    def first(half):
        return 0 if half == 0 else 1

    def piece(slot, half, quarter):
        if quarter is None:
            return kvb.at[half, slot]
        return kvb.at[half, slot, quarter]

    def kv_copy(chunk, half, quarter, send, dest):
        slot = slot_of(chunk, half)
        ref = piece(slot, half, quarter)
        recv = kv_recv.at[slot, half, 0 if quarter is None else quarter]
        return remote(ref, ref, send, recv, (dest, t))

    def base(p):
        return c if p == 0 else mate

    def send_desc(kind, p, r, half, way):
        dim1, dim2 = first(half), 1 - first(half)
        step = 1 - 2 * way
        if kind == "p1a":
            return kv_copy(
                base(p), half, None, kv_send.at[p, 0, half, way], neighbour(c, dim1, step)
            )
        if kind == "p1b":
            chunk = neighbour(base(p), dim1, -step)
            return kv_copy(
                chunk, half, way, kv_send.at[p, 1, half, way], neighbour(c, dim1, step)
            )
        row = neighbour(base(p), dim1, r)
        if kind == "p2a":
            return kv_copy(
                row, half, None, kv_send.at[p, 2 + r, half, way], neighbour(c, dim2, step)
            )
        chunk = neighbour(row, dim2, -step)
        return kv_copy(
            chunk, half, way, kv_send.at[p, 6 + r, half, way], neighbour(c, dim2, step)
        )

    def wait_whole(chunk, half):
        kv_copy(chunk, half, None, kv_send.at[0, 0, 0, 0], c).wait_recv()

    def wait_split(chunk, half):
        for quarter in range(2):
            kv_copy(chunk, half, quarter, kv_send.at[0, 0, 0, 0], c).wait_recv()

    def each(fn):
        for half in range(2):
            for way in range(2):
                fn(half, way)

    def row_sends(p, r):
        each(lambda half, way: send_desc("p2a", p, r, half, way).start())

    def own_sends(p):
        each(lambda half, way: send_desc("p1a", p, 0, half, way).start())

    def own_forwards(p):
        def got_one(half, way):
            wait_whole(neighbour(base(p), first(half), 2 * way - 1), half)
            send_desc("p1b", p, 0, half, way).start()

        each(got_one)

    def far_row(p):
        for half in range(2):
            wait_split(neighbour(base(p), first(half), 2), half)
        row_sends(p, 2)

    def forward(p, r):
        def got_one(half, way):
            row = neighbour(base(p), first(half), r)
            wait_whole(neighbour(row, 1 - first(half), 2 * way - 1), half)
            send_desc("p2b", p, r, half, way).start()

        each(got_one)

    def forwards(p):
        def one(r, carry):
            forward(p, r)
            return carry

        lax.fori_loop(0, 4, one, 0)

    def stage_f(p):
        def one(r, carry):
            for half in range(2):
                row = neighbour(base(p), first(half), r)
                wait_split(neighbour(row, 1 - first(half), 2), half)
            return carry

        lax.fori_loop(0, 4, one, 0)

    def y_copy(half, owner):
        ref = kvb.at[half, slot_of(owner, half)]
        return remote(ref, ref, y_send.at[half], y_recv.at[half], (mate, t))

    following = lax.rem(c + 1, CTX)
    edge_copies = [
        remote(x_ref.at[pl.ds(ROWS - 16, 16)], edge_x, edge_send.at[0], edge_recv.at[0], (following, t)),
        remote(bc_ref.at[pl.ds(ROWS - 16, 16)], edge_bc, edge_send.at[1], edge_recv.at[1], (following, t)),
    ]
    for copy in edge_copies:
        copy.start()
    for half in range(2):
        y_copy(half, c).start()
    own_sends(0)
    row_sends(0, 0)

    for copy in edge_copies:
        copy.wait_recv()

    at_start = c == 0

    def conv(buffer, edge, own_prior, here, taps):
        buffer[5:8, :] = jnp.where(at_start, own_prior, edge.astype(F32)[13:16])
        buffer[8 : 8 + ROWS, :] = here.astype(F32)
        total = taps[0:1] * buffer[5 : 5 + ROWS, :]
        for k in range(1, 4):
            total = total + taps[k : k + 1] * buffer[5 + k : 5 + k + ROWS, :]
        return silu(total)

    flat_prior = prior_bc[...].astype(F32)
    flat_prior = jnp.concatenate([flat_prior[:, 0], flat_prior[:, 1]], axis=1)
    flat_taps = jnp.concatenate([taps_bc[:, 0], taps_bc[:, 1]], axis=1)
    proj = conv(ext_bc, edge_bc[...], flat_prior, bc_ref[...], flat_taps)
    b_ref[...] = proj[:, :NSTATE].astype(BF16)
    c_ref[...] = proj[:, NSTATE:].astype(BF16)
    g_ref[...] = dot(c_ref[...], b_ref[...], NT)

    left_half = lax.broadcasted_iota(jnp.int32, (ROWS, 128), 1) < 64

    def columns(pair):
        return pl.ds(pl.multiple_of(pair * 128, 128), 128)

    def rolled(pair):
        return pltpu.roll(aux[...], 128 - 2 * pair, 1)

    def spread(lanes, at):
        return jnp.where(left_half, lanes[:, at : at + 1], lanes[:, at + 1 : at + 2])

    def mate_copy(q):
        return remote(
            msg.at[pl.ds(theirs + 4 * q, 4)],
            from_mate.at[pl.ds(4 * q, 4)],
            mate_send.at[q],
            mate_recv.at[q],
            (mate, t),
        )

    def decay_rows(total):
        row = lax.broadcasted_iota(jnp.int32, (16, NSTATE), 0)
        hi = total.astype(BF16).astype(F32)
        mid = (total - hi).astype(BF16).astype(F32)
        low = total - hi - mid
        parts = jnp.where(row == 0, hi, jnp.where(row == 1, mid, jnp.where(row == 2, low, 0.0)))
        return parts.astype(BF16)

    def decay_of(rows):
        tail = rows.astype(F32)
        return tail[0:1] + tail[1:2] + tail[2:3]

    def local_states(step, carry):
        pair = lax.rem(step + lax.div(theirs, 2), PAIRS)
        cols = columns(pair)
        act = conv(
            ext, edge_x[:, cols], prior_x[:, cols].astype(F32), x_ref[:, cols], taps_x[:, cols]
        )
        xa[:, cols] = act
        lanes = rolled(pair)
        weighted = (act * spread(lanes, 64)).astype(BF16)
        made = dot(weighted, b_ref[...], TN).astype(BF16)
        for sub in range(2):
            h = 2 * pair + sub
            msg[h, 0:64, :] = made[64 * sub : 64 * sub + 64]
            total = jnp.broadcast_to(lanes[ROWS - 1 : ROWS, sub : sub + 1], (16, NSTATE))
            msg[h, 64:80, :] = decay_rows(total)

        @pl.when((step < 8) & (lax.rem(step, 2) == 1))
        def _():
            mate_copy(lax.div(step, 2)).start()

        @pl.when(step == 2)
        def _():
            own_forwards(0)

        @pl.when(step == 5)
        def _():
            for half in range(2):
                y_copy(half, mate).wait_recv()
            own_sends(1)
            row_sends(0, 1)
            row_sends(0, 3)

        @pl.when(step == 10)
        def _():
            own_forwards(1)
            far_row(0)
            row_sends(1, 0)

        @pl.when(step == 15)
        def _():
            row_sends(1, 1)
            row_sends(1, 3)

        return carry

    lax.fori_loop(0, PAIRS, local_states, 0)
    far_row(1)

    acc[...] = jnp.zeros_like(acc)
    top[...] = jnp.full(top.shape, -1e30, F32)

    lane = lax.broadcasted_iota(jnp.int32, (1, GROUP), 1)
    row_one = lax.broadcasted_iota(jnp.int32, (ROWS, 1), 0)

    def group(half, at, heads_of):
        keys = kvb[half, pl.ds(at * 8, 8), 0].reshape(GROUP, HD)
        vals = kvb[half, pl.ds(at * 8, 8), 1].reshape(GROUP, HD)
        wide = jnp.concatenate([vals, jnp.ones_like(vals)], axis=1)
        if half == 0:
            order = lax.rem(lax.div(lane, ROWS), 4) * 8 + at * 2 + lax.div(lane, 4 * ROWS)
            offset = jnp.where(order < c, ROWS, jnp.where(order == c, 0, -ROWS))
            edge_lane = lax.rem(lane, ROWS) - offset

        def attend(h):
            query = q_ref[:, pl.ds(pl.multiple_of(h * HD, HD), HD)]
            scores = dot(query, keys, NT)
            if half == 0:
                scores = jnp.where(edge_lane <= row_one, scores, -1e30)
            return scores

        def absorb(h, scores):
            before = top[h]
            new = jnp.maximum(before, jnp.max(scores, axis=1, keepdims=True))
            top[h] = new
            shrink = jnp.exp2((before - new) * COEF)
            weights = jnp.exp2((scores - new[:, 0:1]) * COEF).astype(BF16)
            acc[h] = acc[h] * jnp.concatenate([shrink, shrink], axis=1) + dot(weights, wide)

        ahead = attend(heads_of[0])
        for i, h in enumerate(heads_of):
            scores = ahead
            if i + 1 < len(heads_of):
                ahead = attend(heads_of[i + 1])
            absorb(h, scores)

    prior_copy.wait()

    def pair_copy(i, source):
        return remote(
            comb.at[i], got.at[source], st_send.at[i], st_recv.at[source], (2 * i + side, t)
        )

    def back_copy(j, owner):
        return remote(
            back.at[j], inc_pair.at[owner], in_send.at[j], in_recv.at[owner], (2 * j + side, t)
        )

    def out_copy(q, half_at):
        return remote(
            out_mate.at[pl.ds(pl.multiple_of(q * 256, 256), 256)],
            incoming.at[pl.ds(pl.multiple_of(half_at * 64 + q * 256, 256), 256)],
            out_send.at[q],
            out_recv.at[q],
            (mate, t),
        )

    def earlier_of(i):
        own_total = decay_of(msg[mine + i, 64:80, :])
        mate_total = decay_of(from_mate[i, 64:80, :])
        own_state = msg[mine + i, 0:64, :].astype(F32)
        mate_state = from_mate[i, 0:64, :].astype(F32)
        first_side = side == 0
        return (
            jnp.where(first_side, own_total, mate_total),
            jnp.where(first_side, own_state, mate_state),
            jnp.where(first_side, mate_total, own_total),
            jnp.where(first_side, mate_state, own_state),
        )

    def combine(step, carry):
        i = lax.rem(spot + step, SPOTS)
        early_total, early_state, late_total, late_state = earlier_of(i)
        comb[i, 0:64, :] = (jnp.exp(late_total) * early_state + late_state).astype(BF16)
        comb[i, 64:80, :] = decay_rows(jnp.broadcast_to(early_total + late_total, (16, NSTATE)))

        @pl.when(step != 0)
        def _():
            pair_copy(i, spot).start()

        @pl.when(step == 0)
        def _():
            got[spot] = comb[i]

        return carry

    def scan(j, carry):
        @pl.when(j != spot)
        def _():
            pair_copy(j, j).wait_recv()

        now = state[...]
        back[j] = now.astype(BF16)
        state[...] = jnp.exp(decay_of(got[j, 64:80, :])) * now + got[j, 0:64, :].astype(F32)
        return carry

    def give_back(i, carry):
        back_copy(lax.rem(spot + i, SPOTS), spot).start()
        return carry

    def settle(i, carry):
        @pl.when(i != spot)
        def _():
            back_copy(i, i).wait_recv()

        early_total, early_state, _, _ = earlier_of(i)
        entering = inc_pair[i].astype(F32)
        after = jnp.exp(early_total) * entering + early_state
        rows = pl.ds(pl.multiple_of((mine + i) * 64, 64), 64)
        incoming[rows, :] = jnp.where(side == 0, entering, after).astype(BF16)
        out_mate[pl.ds(pl.multiple_of(i * 64, 64), 64), :] = jnp.where(
            side == 0, after, entering
        ).astype(BF16)

        @pl.when(lax.rem(i, 4) == 3)
        def _():
            out_copy(lax.div(i, 4), mine).start()

        return carry

    def within_block(pair, carry):
        cols = columns(pair)
        lanes = rolled(pair)
        act = xa[:, cols]
        scaled = (act * spread(lanes, 32)).astype(BF16)
        skips = jnp.where(left_half, skip_ref[2 * pair], skip_ref[2 * pair + 1])
        parts = []
        for sub in range(2):
            h = 2 * pair + sub
            diff = lanes[:, sub : sub + 1] - cum_t[pl.ds(h, 1), :]
            decay = jnp.exp(jnp.where(lower, diff, -1e30))
            parts.append(dot((g_ref[...] * decay).astype(BF16), scaled))
        xa[:, cols] = jnp.where(left_half, parts[0], parts[1]) + skips * act

        return carry


    def at_of(half, far):
        here = lax.div(c, 8) if half == 1 else lax.rem(lax.div(c, 2), 4)
        return lax.rem(here + far, 4)

    def near(g, carry):
        far = jnp.where(g == 2, 3, g)

        @pl.when(g == 1)
        def _():
            lax.fori_loop(0, PAIRS, within_block, 0)
            forwards(1)

        group(1, at_of(1, far), list(range(HEADS)))

        @pl.when(g == 0)
        def _():
            forwards(0)
            for q in range(4):
                mate_copy(q).wait_recv()
            lax.fori_loop(0, SPOTS, combine, 0)

        @pl.when(g == 1)
        def _():
            lax.fori_loop(0, SPOTS, scan, 0)
            inc_pair[spot] = back[spot]
            lax.fori_loop(1, SPOTS, give_back, 0)

        @pl.when(g == 2)
        def _():
            lax.fori_loop(0, SPOTS, settle, 0)

        group(0, at_of(0, far), list(range(HEADS)))
        return carry

    lax.fori_loop(0, 3, near, 0)
    stage_f(0)
    stage_f(1)

    other_core = t + 1 - 2 * lax.rem(t, 2)
    across = lax.rem(t + 2, TP)

    def head_copy(src, h, dest, kind):
        cols = pl.ds(pl.multiple_of((src * HEADS + h) * HD, HD), HD)
        return remote(
            heads.at[:, cols], heads.at[:, cols], hd_send.at[h, kind], hd_recv.at[src, h], (c, dest)
        )

    def pass_on(h, carry):
        head_copy(across, h, across, 0).wait_recv()
        head_copy(across, h, other_core, 2).start()
        return carry

    def last(part, carry):
        heads_of = [part * 4 + i for i in range(4)]
        group(1, at_of(1, 2), heads_of)
        group(0, at_of(0, 2), heads_of)
        for h in heads_of:
            full = acc[h]
            cols = pl.ds(pl.multiple_of((t * HEADS + h) * HD, HD), HD)
            heads[:, cols] = (full[:, :HD] / full[:, HD:]).astype(BF16)
            head_copy(t, h, across, 0).start()
            head_copy(t, h, other_core, 1).start()
        return carry

    lax.fori_loop(0, 2, last, 0)
    lax.fori_loop(0, 4, pass_on, 0)

    for q in range(4):
        out_copy(q, theirs).wait_recv()
    squares[...] = jnp.zeros_like(squares)

    def mix(pair, carry):
        cols = columns(pair)
        lanes = rolled(pair)
        earlier = dot(c_ref[...], incoming[cols, :], NT)
        mixed = xa[:, cols] + spread(lanes, 96) * earlier
        gated = mixed * silu(z_ref[:, cols].astype(F32))
        squares[...] += gated * gated
        xa[:, cols] = gated
        return carry

    lax.fori_loop(0, PAIRS, mix, 0)
    mean = jnp.sum(squares[...], axis=1, keepdims=True) * (1.0 / WIDE)
    squares[...] = jnp.broadcast_to(lax.rsqrt(mean + 1e-05), squares.shape)

    def norm(pair, carry):
        cols = columns(pair)
        ssm_ref[:, cols] = (xa[:, cols] * squares[...] * gain_ref[:, cols]).astype(BF16)
        return carry

    lax.fori_loop(0, PAIRS, norm, 0)

    lax.fori_loop(4, HEADS, pass_on, 0)

    def head_wait(h, carry):
        head_copy(other_core, h, other_core, 1).wait_recv()
        head_copy(lax.rem(other_core + 2, TP), h, other_core, 2).wait_recv()
        return carry

    lax.fori_loop(0, HEADS, head_wait, 0)
    w_copy.wait()

    def project(n, carry):
        cols = pl.ds(pl.multiple_of(n * 256, 256), 256)
        attn_ref[:, cols] = dot(heads[...], w_ref[:, cols]).astype(BF16)
        return carry

    lax.fori_loop(0, WIDE // 256, project, 0)

    for copy in edge_copies:
        copy.wait_send()
    for half in range(2):
        y_copy(half, c).wait_send()
    for p in range(2):
        each(lambda half, way: send_desc("p1a", p, 0, half, way).wait_send())
        each(lambda half, way: send_desc("p1b", p, 0, half, way).wait_send())

        def sent(r, carry):
            each(lambda half, way: send_desc("p2a", p, r, half, way).wait_send())
            each(lambda half, way: send_desc("p2b", p, r, half, way).wait_send())
            return carry

        lax.fori_loop(0, 4, sent, 0)

    for q in range(4):
        mate_copy(q).wait_send()
        out_copy(q, mine).wait_send()

    def states_sent(step, carry):
        i = lax.rem(spot + step, SPOTS)
        pair_copy(i, spot).wait_send()
        back_copy(i, spot).wait_send()
        return carry

    lax.fori_loop(1, SPOTS, states_sent, 0)

    def heads_sent(h, carry):
        head_copy(t, h, across, 0).wait_send()
        head_copy(t, h, other_core, 1).wait_send()
        head_copy(across, h, other_core, 2).wait_send()
        return carry

    lax.fori_loop(0, HEADS, heads_sent, 0)


def per_device(
    queries,
    keys,
    values,
    prior_keys,
    prior_values,
    out_weight,
    ssm_x,
    ssm_bc,
    gate_z,
    conv_x,
    conv_bc,
    conv_prior_x,
    conv_prior_bc,
    step_dt,
    log_decay,
    skip_d,
    ssm_prior,
    norm_gain,
):
    vm = pl.BlockSpec(memory_space=pltpu.VMEM)
    anywhere = pl.BlockSpec(memory_space=pl.ANY)
    small = pl.BlockSpec(memory_space=pltpu.SMEM)
    return pl.pallas_call(
        kernel,
        out_shape=(
            jax.ShapeDtypeStruct((ROWS, WIDE), BF16),
            jax.ShapeDtypeStruct((ROWS, WIDE), BF16),
        ),
        in_specs=[vm] * 5 + [anywhere] + [vm] * 9 + [small, anywhere, vm],
        out_specs=(vm, vm),
        scratch_shapes=[
            pltpu.VMEM((2, CTX, 2, ROWS, HD), BF16),
            pltpu.VMEM((HEADS, ROWS, 2 * HD), F32),
            pltpu.VMEM((HEADS, ROWS, HD), F32),
            pltpu.VMEM((ROWS, TP * HEADS * HD), BF16),
            pltpu.VMEM((TP * HEADS * HD, WIDE), BF16),
            pltpu.VMEM((16, WIDE), BF16),
            pltpu.VMEM((16, 2 * NSTATE), BF16),
            pltpu.VMEM((ROWS + 8, 128), F32),
            pltpu.VMEM((ROWS + 8, 2 * NSTATE), F32),
            pltpu.VMEM((ROWS, NSTATE), BF16),
            pltpu.VMEM((ROWS, NSTATE), BF16),
            pltpu.VMEM((ROWS, ROWS), F32),
            pltpu.VMEM((ROWS, 128), F32),
            pltpu.VMEM((SH, ROWS), F32),
            pltpu.VMEM((ROWS, WIDE), F32),
            pltpu.VMEM((SH, MSG, NSTATE), BF16),
            pltpu.VMEM((SPOTS, MSG, NSTATE), BF16),
            pltpu.VMEM((SPOTS, MSG, NSTATE), BF16),
            pltpu.VMEM((SPOTS, MSG, NSTATE), BF16),
            pltpu.VMEM((64, NSTATE), F32),
            pltpu.VMEM((SPOTS, 64, NSTATE), BF16),
            pltpu.VMEM((SPOTS, 64, NSTATE), BF16),
            pltpu.VMEM((SPOTS * 64, NSTATE), BF16),
            pltpu.VMEM((WIDE, NSTATE), BF16),
            pltpu.VMEM((ROWS, 128), F32),
            pltpu.SemaphoreType.DMA,
            pltpu.SemaphoreType.DMA,
            pltpu.SemaphoreType.DMA((2,)),
            pltpu.SemaphoreType.DMA((2,)),
            pltpu.SemaphoreType.DMA((2, 10, 2, 2)),
            pltpu.SemaphoreType.DMA((CTX, 2, 2)),
            pltpu.SemaphoreType.DMA((2,)),
            pltpu.SemaphoreType.DMA((2,)),
            pltpu.SemaphoreType.DMA((4,)),
            pltpu.SemaphoreType.DMA((4,)),
            pltpu.SemaphoreType.DMA((SPOTS,)),
            pltpu.SemaphoreType.DMA((SPOTS,)),
            pltpu.SemaphoreType.DMA((SPOTS,)),
            pltpu.SemaphoreType.DMA((SPOTS,)),
            pltpu.SemaphoreType.DMA((4,)),
            pltpu.SemaphoreType.DMA((4,)),
            pltpu.SemaphoreType.DMA((HEADS, 3)),
            pltpu.SemaphoreType.DMA((TP, HEADS)),
        ],
        compiler_params=pltpu.CompilerParams(
            collective_id=0, has_side_effects=True, vmem_limit_bytes=60 * 2**20
        ),
        name="hybrid",
    )(
        queries,
        keys,
        values,
        prior_keys,
        prior_values,
        out_weight,
        ssm_x,
        ssm_bc.reshape(ROWS, 2 * NSTATE),
        gate_z,
        conv_x,
        conv_bc,
        conv_prior_x,
        conv_prior_bc,
        step_dt.T,
        log_decay.T,
        skip_d,
        ssm_prior.reshape(WIDE, NSTATE),
        norm_gain.reshape(1, WIDE),
    )


def solution(mesh):
    in_specs = (
        P("ctx", "tp"),
        P("ctx", "tp"),
        P("ctx", "tp"),
        P("ctx", "tp"),
        P("ctx", "tp"),
        P(None, "tp"),
        P("ctx", "tp"),
        P("ctx", None, "tp"),
        P("ctx", "tp"),
        P(None, "tp"),
        P(None, None, "tp"),
        P(None, "tp"),
        P(None, None, "tp"),
        P("ctx", "tp"),
        P("ctx", "tp"),
        P("tp"),
        P("tp", None, None),
        P("tp"),
    )
    out_specs = (P("ctx", "tp"), P("ctx", "tp"))
    return jax.shard_map(
        per_device, mesh=mesh, in_specs=in_specs, out_specs=out_specs, check_vma=False
    )
```

```python
import functools

import jax
import jax.numpy as jnp
from jax import lax
from jax.experimental import pallas as pl
from jax.experimental.pallas import tpu as pltpu
from jax.sharding import PartitionSpec as P

MESH = pl.DeviceIdType.MESH
F32 = jnp.float32
BF16 = jnp.bfloat16
HD = 128
CTX = 32
TP = 4
ROWS = 256
HEADS = 8
SH = 32
WIDE = 2048
PAIRS = 16
NSTATE = 256
MSG = 80
GROUP = 8 * ROWS
SPOTS = CTX // 2
COEF = 1.4426950408889634 / (HD**0.5)
NT = (((1,), (1,)), ((), ()))
TN = (((0,), (0,)), ((), ()))


def dot(a, b, dims=(((1,), (0,)), ((), ()))):
    return lax.dot_general(a, b, dims, preferred_element_type=F32)


def exact_dot(a, b, dims):
    return lax.dot_general(
        a, b, dims, preferred_element_type=F32, precision=lax.Precision.HIGHEST
    )


def silu(v):
    return v / (1.0 + jnp.exp(-v))


def neighbour(c, dim, step):
    if dim == 0:
        return lax.rem(c + 8 * step + 32, 32)
    z = lax.rem(lax.div(c, 2), 4)
    return c + 2 * (lax.rem(z + step + 4, 4) - z)


def slot_of(c, half):
    x, z, y = lax.div(c, 8), lax.rem(lax.div(c, 2), 4), lax.rem(c, 2)
    return z * 8 + y * 4 + x if half == 0 else x * 8 + y * 4 + z


def kernel(
    q_ref,
    k_ref,
    v_ref,
    pk_ref,
    pv_ref,
    w_hbm,
    x_ref,
    bc_ref,
    z_ref,
    taps_x,
    taps_bc,
    prior_x,
    prior_bc,
    dt_ref,
    ld_ref,
    skip_ref,
    prior_hbm,
    gain_ref,
    attn_ref,
    ssm_ref,
    kvb,
    acc,
    top,
    heads,
    w_ref,
    edge_x,
    edge_bc,
    ext,
    ext_bc,
    b_ref,
    c_ref,
    g_ref,
    aux,
    cum_t,
    xa,
    msg,
    from_mate,
    comb,
    got,
    state,
    back,
    inc_pair,
    out_mate,
    incoming,
    squares,
    w_sem,
    prior_sem,
    y_send,
    y_recv,
    kv_send,
    kv_recv,
    edge_send,
    edge_recv,
    mate_send,
    mate_recv,
    st_send,
    st_recv,
    in_send,
    in_recv,
    out_send,
    out_recv,
    hd_send,
    hd_recv,
):
    c = lax.axis_index("ctx")
    t = lax.axis_index("tp")
    side = lax.rem(c, 2)
    spot = lax.div(c, 2)
    mate = c + 1 - 2 * side
    mine = SPOTS * side
    theirs = SPOTS * (1 - side)

    def remote(src, dst, send, recv, dev):
        return pltpu.make_async_remote_copy(
            src_ref=src,
            dst_ref=dst,
            send_sem=send,
            recv_sem=recv,
            device_id=dev,
            device_id_type=MESH,
        )

    w_copy = pltpu.make_async_copy(w_hbm, w_ref, w_sem)
    w_copy.start()
    prior_copy = pltpu.make_async_copy(
        prior_hbm.at[pl.ds(pl.multiple_of((mine + spot) * 64, 64), 64)], state, prior_sem
    )
    prior_copy.start()
    barrier = pltpu.get_barrier_semaphore()

    def greet(dev):
        pl.semaphore_signal(barrier, inc=1, device_id=dev, device_id_type=MESH)

    def greet_ctx(i, carry):
        greet((2 * lax.rem(spot + i, SPOTS) + side, t))
        return carry

    lax.fori_loop(1, SPOTS, greet_ctx, 0)
    greet((mate, t))
    greet((lax.rem(c + 2 * side - 1 + CTX, CTX), t))
    greet((c, t + 1 - 2 * lax.rem(t, 2)))
    greet((c, lax.rem(t + 2, TP)))
    kvb[0, slot_of(c, 0), 0] = k_ref[...]
    kvb[0, slot_of(c, 0), 1] = v_ref[...]
    kvb[1, slot_of(c, 1), 0] = pk_ref[...]
    kvb[1, slot_of(c, 1), 1] = pv_ref[...]

    row_i = lax.broadcasted_iota(jnp.int32, (ROWS, ROWS), 0)
    col_i = lax.broadcasted_iota(jnp.int32, (ROWS, ROWS), 1)
    lower = row_i >= col_i
    ones_low = jnp.where(lower, 1.0, 0.0).astype(F32)
    ld = ld_ref[...]
    cum = exact_dot(ones_low, ld, NT)
    cum_t[...] = exact_dot(ld, ones_low, NT)
    dt = exact_dot(jnp.where(row_i == col_i, 1.0, 0.0).astype(F32), dt_ref[...], NT)
    aux[:, 0:32] = cum
    aux[:, 32:64] = dt
    aux[:, 64:96] = jnp.exp(cum[ROWS - 1 : ROWS] - cum) * dt
    aux[:, 96:128] = jnp.exp(cum)

    pl.semaphore_wait(barrier, SPOTS + 3)

    def first(half):
        return 0 if half == 0 else 1

    def piece(slot, half, quarter):
        if quarter is None:
            return kvb.at[half, slot]
        return kvb.at[half, slot, quarter]

    def kv_copy(chunk, half, quarter, send, dest):
        slot = slot_of(chunk, half)
        ref = piece(slot, half, quarter)
        recv = kv_recv.at[slot, half, 0 if quarter is None else quarter]
        return remote(ref, ref, send, recv, (dest, t))

    def base(p):
        return c if p == 0 else mate

    def send_desc(kind, p, r, half, way):
        dim1, dim2 = first(half), 1 - first(half)
        step = 1 - 2 * way
        if kind == "p1a":
            return kv_copy(
                base(p), half, None, kv_send.at[p, 0, half, way], neighbour(c, dim1, step)
            )
        if kind == "p1b":
            chunk = neighbour(base(p), dim1, -step)
            return kv_copy(
                chunk, half, way, kv_send.at[p, 1, half, way], neighbour(c, dim1, step)
            )
        row = neighbour(base(p), dim1, r)
        if kind == "p2a":
            return kv_copy(
                row, half, None, kv_send.at[p, 2 + r, half, way], neighbour(c, dim2, step)
            )
        chunk = neighbour(row, dim2, -step)
        return kv_copy(
            chunk, half, way, kv_send.at[p, 6 + r, half, way], neighbour(c, dim2, step)
        )

    def wait_whole(chunk, half):
        kv_copy(chunk, half, None, kv_send.at[0, 0, 0, 0], c).wait_recv()

    def wait_split(chunk, half):
        for quarter in range(2):
            kv_copy(chunk, half, quarter, kv_send.at[0, 0, 0, 0], c).wait_recv()

    def each(fn):
        for half in range(2):
            for way in range(2):
                fn(half, way)

    def row_sends(p, r):
        each(lambda half, way: send_desc("p2a", p, r, half, way).start())

    def own_sends(p):
        each(lambda half, way: send_desc("p1a", p, 0, half, way).start())

    def own_forwards(p):
        def got_one(half, way):
            wait_whole(neighbour(base(p), first(half), 2 * way - 1), half)
            send_desc("p1b", p, 0, half, way).start()

        each(got_one)

    def far_row(p):
        for half in range(2):
            wait_split(neighbour(base(p), first(half), 2), half)
        row_sends(p, 2)

    def forward(p, r):
        def got_one(half, way):
            row = neighbour(base(p), first(half), r)
            wait_whole(neighbour(row, 1 - first(half), 2 * way - 1), half)
            send_desc("p2b", p, r, half, way).start()

        each(got_one)

    def forwards(p):
        def one(r, carry):
            forward(p, r)
            return carry

        lax.fori_loop(0, 4, one, 0)

    def stage_f(p):
        def one(r, carry):
            for half in range(2):
                row = neighbour(base(p), first(half), r)
                wait_split(neighbour(row, 1 - first(half), 2), half)
            return carry

        lax.fori_loop(0, 4, one, 0)

    def y_copy(half, owner):
        ref = kvb.at[half, slot_of(owner, half)]
        return remote(ref, ref, y_send.at[half], y_recv.at[half], (mate, t))

    following = lax.rem(c + 1, CTX)
    edge_copies = [
        remote(x_ref.at[pl.ds(ROWS - 16, 16)], edge_x, edge_send.at[0], edge_recv.at[0], (following, t)),
        remote(bc_ref.at[pl.ds(ROWS - 16, 16)], edge_bc, edge_send.at[1], edge_recv.at[1], (following, t)),
    ]
    for copy in edge_copies:
        copy.start()
    for half in range(2):
        y_copy(half, c).start()
    own_sends(0)
    row_sends(0, 0)

    for copy in edge_copies:
        copy.wait_recv()

    at_start = c == 0

    def conv(buffer, edge, own_prior, here, taps):
        buffer[5:8, :] = jnp.where(at_start, own_prior, edge.astype(F32)[13:16])
        buffer[8 : 8 + ROWS, :] = here.astype(F32)
        total = taps[0:1] * buffer[5 : 5 + ROWS, :]
        for k in range(1, 4):
            total = total + taps[k : k + 1] * buffer[5 + k : 5 + k + ROWS, :]
        return silu(total)

    flat_prior = prior_bc[...].astype(F32)
    flat_prior = jnp.concatenate([flat_prior[:, 0], flat_prior[:, 1]], axis=1)
    flat_taps = jnp.concatenate([taps_bc[:, 0], taps_bc[:, 1]], axis=1)
    proj = conv(ext_bc, edge_bc[...], flat_prior, bc_ref[...], flat_taps)
    b_ref[...] = proj[:, :NSTATE].astype(BF16)
    c_ref[...] = proj[:, NSTATE:].astype(BF16)
    g_ref[...] = dot(c_ref[...], b_ref[...], NT)

    left_half = lax.broadcasted_iota(jnp.int32, (ROWS, 128), 1) < 64

    def columns(pair):
        return pl.ds(pl.multiple_of(pair * 128, 128), 128)

    def rolled(pair):
        return pltpu.roll(aux[...], 128 - 2 * pair, 1)

    def spread(lanes, at):
        return jnp.where(left_half, lanes[:, at : at + 1], lanes[:, at + 1 : at + 2])

    def mate_copy(q):
        return remote(
            msg.at[pl.ds(theirs + 4 * q, 4)],
            from_mate.at[pl.ds(4 * q, 4)],
            mate_send.at[q],
            mate_recv.at[q],
            (mate, t),
        )

    def decay_rows(total):
        row = lax.broadcasted_iota(jnp.int32, (16, NSTATE), 0)
        hi = total.astype(BF16).astype(F32)
        mid = (total - hi).astype(BF16).astype(F32)
        low = total - hi - mid
        parts = jnp.where(row == 0, hi, jnp.where(row == 1, mid, jnp.where(row == 2, low, 0.0)))
        return parts.astype(BF16)

    def decay_of(rows):
        tail = rows.astype(F32)
        return tail[0:1] + tail[1:2] + tail[2:3]

    def local_pair(pair, buffer):
        cols = columns(pair)
        act = conv(
            buffer, edge_x[:, cols], prior_x[:, cols].astype(F32), x_ref[:, cols], taps_x[:, cols]
        )
        xa[:, cols] = act
        lanes = rolled(pair)
        weighted = (act * spread(lanes, 64)).astype(BF16)
        made = dot(weighted, b_ref[...], TN).astype(BF16)
        for sub in range(2):
            h = 2 * pair + sub
            msg[h, 0:64, :] = made[64 * sub : 64 * sub + 64]
            total = jnp.broadcast_to(lanes[ROWS - 1 : ROWS, sub : sub + 1], (16, NSTATE))
            msg[h, 64:80, :] = decay_rows(total)

    def local_states(step, carry):
        pair = lax.rem(2 * step + lax.div(theirs, 2), PAIRS)
        local_pair(pair, ext.at[0])
        local_pair(pair + 1, ext.at[1])

        @pl.when(step < 4)
        def _():
            mate_copy(step).start()

        @pl.when(step == 1)
        def _():
            own_forwards(0)
            row_sends(0, 1)
            row_sends(0, 3)

        @pl.when(step == 4)
        def _():
            for half in range(2):
                y_copy(half, mate).wait_recv()
            own_sends(1)

        return carry

    lax.fori_loop(0, PAIRS // 2, local_states, 0)
    far_row(0)
    row_sends(1, 0)

    def within_pair(pair):
        cols = columns(pair)
        lanes = rolled(pair)
        act = xa[:, cols]
        scaled = (act * spread(lanes, 32)).astype(BF16)
        skips = jnp.where(left_half, skip_ref[2 * pair], skip_ref[2 * pair + 1])
        parts = []
        for sub in range(2):
            h = 2 * pair + sub
            diff = lanes[:, sub : sub + 1] - cum_t[pl.ds(h, 1), :]
            decay = jnp.exp(jnp.where(lower, diff, -1e30))
            parts.append(dot((g_ref[...] * decay).astype(BF16), scaled))
        return jnp.where(left_half, parts[0], parts[1]) + skips * act

    def within_block(i, carry):
        results = [within_pair(2 * i), within_pair(2 * i + 1)]
        for sub in range(2):
            xa[:, columns(2 * i + sub)] = results[sub]

        @pl.when(i == 0)
        def _():
            own_forwards(1)
            row_sends(1, 1)
            row_sends(1, 3)

        return carry

    lax.fori_loop(0, PAIRS // 2, within_block, 0)
    far_row(1)
    forwards(0)


    acc[...] = jnp.zeros_like(acc)
    top[...] = jnp.full(top.shape, -1e30, F32)

    lane = lax.broadcasted_iota(jnp.int32, (1, GROUP), 1)
    row_one = lax.broadcasted_iota(jnp.int32, (ROWS, 1), 0)

    def group(*runs):
        units = []
        for half, at, heads_of in runs:
            keys = kvb[half, pl.ds(at * 8, 8), 0].reshape(GROUP, HD)
            vals = kvb[half, pl.ds(at * 8, 8), 1].reshape(GROUP, HD)
            wide = jnp.concatenate([vals, jnp.ones_like(vals)], axis=1)
            edge_lane = None
            if half == 0:
                order = lax.rem(lax.div(lane, ROWS), 4) * 8 + at * 2 + lax.div(lane, 4 * ROWS)
                offset = jnp.where(order < c, ROWS, jnp.where(order == c, 0, -ROWS))
                edge_lane = lax.rem(lane, ROWS) - offset
            units += [(h, keys, wide, edge_lane) for h in heads_of]

        def attend(h, keys, wide, edge_lane):
            query = q_ref[:, pl.ds(pl.multiple_of(h * HD, HD), HD)]
            scores = dot(query, keys, NT)
            if edge_lane is not None:
                scores = jnp.where(edge_lane <= row_one, scores, -1e30)
            return scores

        def absorb(h, wide, scores):
            before = top[h]
            new = jnp.maximum(before, jnp.max(scores, axis=1, keepdims=True))
            top[h] = new
            shrink = jnp.exp2((before - new) * COEF)
            weights = jnp.exp2((scores - new[:, 0:1]) * COEF).astype(BF16)
            acc[h] = acc[h] * jnp.concatenate([shrink, shrink], axis=1) + dot(weights, wide)

        ahead = attend(*units[0])
        for i, unit in enumerate(units):
            scores = ahead
            if i + 1 < len(units):
                ahead = attend(*units[i + 1])
            absorb(unit[0], unit[2], scores)

    prior_copy.wait()

    def pair_copy(i, source):
        return remote(
            comb.at[i], got.at[source], st_send.at[i], st_recv.at[source], (2 * i + side, t)
        )

    def back_copy(j, owner):
        return remote(
            back.at[j], inc_pair.at[owner], in_send.at[j], in_recv.at[owner], (2 * j + side, t)
        )

    def out_copy(q, half_at):
        return remote(
            out_mate.at[pl.ds(pl.multiple_of(q * 256, 256), 256)],
            incoming.at[pl.ds(pl.multiple_of(half_at * 64 + q * 256, 256), 256)],
            out_send.at[q],
            out_recv.at[q],
            (mate, t),
        )

    def earlier_of(i):
        own_total = decay_of(msg[mine + i, 64:80, :])
        mate_total = decay_of(from_mate[i, 64:80, :])
        own_state = msg[mine + i, 0:64, :].astype(F32)
        mate_state = from_mate[i, 0:64, :].astype(F32)
        first_side = side == 0
        return (
            jnp.where(first_side, own_total, mate_total),
            jnp.where(first_side, own_state, mate_state),
            jnp.where(first_side, mate_total, own_total),
            jnp.where(first_side, mate_state, own_state),
        )

    def combine(step, carry):
        i = lax.rem(spot + step, SPOTS)
        early_total, early_state, late_total, late_state = earlier_of(i)
        comb[i, 0:64, :] = (jnp.exp(late_total) * early_state + late_state).astype(BF16)
        comb[i, 64:80, :] = decay_rows(jnp.broadcast_to(early_total + late_total, (16, NSTATE)))

        @pl.when(step != 0)
        def _():
            pair_copy(i, spot).start()

        @pl.when(step == 0)
        def _():
            got[spot] = comb[i]

        return carry

    def scan(j, carry):
        @pl.when(j != spot)
        def _():
            pair_copy(j, j).wait_recv()

        now = state[...]
        back[j] = now.astype(BF16)
        state[...] = jnp.exp(decay_of(got[j, 64:80, :])) * now + got[j, 0:64, :].astype(F32)
        return carry

    def give_back(i, carry):
        back_copy(lax.rem(spot + i, SPOTS), spot).start()
        return carry

    def settle(i, carry):
        @pl.when(i != spot)
        def _():
            back_copy(i, i).wait_recv()

        early_total, early_state, _, _ = earlier_of(i)
        entering = inc_pair[i].astype(F32)
        after = jnp.exp(early_total) * entering + early_state
        rows = pl.ds(pl.multiple_of((mine + i) * 64, 64), 64)
        incoming[rows, :] = jnp.where(side == 0, entering, after).astype(BF16)
        out_mate[pl.ds(pl.multiple_of(i * 64, 64), 64), :] = jnp.where(
            side == 0, after, entering
        ).astype(BF16)

        @pl.when(lax.rem(i, 4) == 3)
        def _():
            out_copy(lax.div(i, 4), mine).start()

        return carry

    def at_of(half, far):
        here = lax.div(c, 8) if half == 1 else lax.rem(lax.div(c, 2), 4)
        return lax.rem(here + far, 4)

    def near(g, carry):
        far = jnp.where(g == 2, 3, g)

        group((1, at_of(1, far), list(range(HEADS))))

        @pl.when(g == 0)
        def _():
            for q in range(4):
                mate_copy(q).wait_recv()
            lax.fori_loop(0, SPOTS, combine, 0)
            forwards(1)

        @pl.when(g == 1)
        def _():
            lax.fori_loop(0, SPOTS, scan, 0)
            inc_pair[spot] = back[spot]
            lax.fori_loop(1, SPOTS, give_back, 0)

        @pl.when(g == 2)
        def _():
            lax.fori_loop(0, SPOTS, settle, 0)

        group((0, at_of(0, far), list(range(HEADS))))
        return carry

    lax.fori_loop(0, 3, near, 0)
    stage_f(0)
    stage_f(1)

    other_core = t + 1 - 2 * lax.rem(t, 2)
    across = lax.rem(t + 2, TP)

    def head_copy(src, h, dest, kind):
        cols = pl.ds(pl.multiple_of((src * HEADS + h) * HD, HD), HD)
        return remote(
            heads.at[:, cols], heads.at[:, cols], hd_send.at[h, kind], hd_recv.at[src, h], (c, dest)
        )

    def pass_on(h, carry):
        head_copy(across, h, across, 0).wait_recv()
        head_copy(across, h, other_core, 2).start()
        return carry

    def last(part, carry):
        heads_of = [part * 4 + i for i in range(4)]
        group((1, at_of(1, 2), heads_of), (0, at_of(0, 2), heads_of))
        for h in heads_of:
            full = acc[h]
            cols = pl.ds(pl.multiple_of((t * HEADS + h) * HD, HD), HD)
            heads[:, cols] = (full[:, :HD] / full[:, HD:]).astype(BF16)
            head_copy(t, h, across, 0).start()
            head_copy(t, h, other_core, 1).start()
        return carry

    lax.fori_loop(0, 2, last, 0)
    lax.fori_loop(0, 4, pass_on, 0)

    for q in range(4):
        out_copy(q, theirs).wait_recv()
    squares[...] = jnp.zeros_like(squares)

    def mix_pair(pair):
        cols = columns(pair)
        lanes = rolled(pair)
        earlier = dot(c_ref[...], incoming[cols, :], NT)
        mixed = xa[:, cols] + spread(lanes, 96) * earlier
        return mixed * silu(z_ref[:, cols].astype(F32))

    def mix(i, carry):
        results = [mix_pair(4 * i + sub) for sub in range(4)]
        parts = [gated * gated for gated in results]
        squares[...] += (parts[0] + parts[1]) + (parts[2] + parts[3])
        for sub in range(4):
            xa[:, columns(4 * i + sub)] = results[sub]
        return carry

    lax.fori_loop(0, PAIRS // 4, mix, 0)
    mean = jnp.sum(squares[...], axis=1, keepdims=True) * (1.0 / WIDE)
    squares[...] = jnp.broadcast_to(lax.rsqrt(mean + 1e-05), squares.shape)

    def norm(i, carry):
        for sub in range(4):
            cols = columns(4 * i + sub)
            ssm_ref[:, cols] = (xa[:, cols] * squares[...] * gain_ref[:, cols]).astype(BF16)
        return carry

    lax.fori_loop(0, PAIRS // 4, norm, 0)

    lax.fori_loop(4, HEADS, pass_on, 0)

    def head_wait(h, carry):
        head_copy(other_core, h, other_core, 1).wait_recv()
        head_copy(lax.rem(other_core + 2, TP), h, other_core, 2).wait_recv()
        return carry

    lax.fori_loop(0, HEADS, head_wait, 0)
    w_copy.wait()

    def project(n, carry):
        cols = pl.ds(pl.multiple_of(n * 256, 256), 256)
        attn_ref[:, cols] = dot(heads[...], w_ref[:, cols]).astype(BF16)
        return carry

    lax.fori_loop(0, WIDE // 256, project, 0)

    for copy in edge_copies:
        copy.wait_send()
    for half in range(2):
        y_copy(half, c).wait_send()
    for p in range(2):
        each(lambda half, way: send_desc("p1a", p, 0, half, way).wait_send())
        each(lambda half, way: send_desc("p1b", p, 0, half, way).wait_send())

        def sent(r, carry):
            each(lambda half, way: send_desc("p2a", p, r, half, way).wait_send())
            each(lambda half, way: send_desc("p2b", p, r, half, way).wait_send())
            return carry

        lax.fori_loop(0, 4, sent, 0)

    for q in range(4):
        mate_copy(q).wait_send()
        out_copy(q, mine).wait_send()

    def states_sent(step, carry):
        i = lax.rem(spot + step, SPOTS)
        pair_copy(i, spot).wait_send()
        back_copy(i, spot).wait_send()
        return carry

    lax.fori_loop(1, SPOTS, states_sent, 0)

    def heads_sent(h, carry):
        head_copy(t, h, across, 0).wait_send()
        head_copy(t, h, other_core, 1).wait_send()
        head_copy(across, h, other_core, 2).wait_send()
        return carry

    lax.fori_loop(0, HEADS, heads_sent, 0)


def per_device(
    queries,
    keys,
    values,
    prior_keys,
    prior_values,
    out_weight,
    ssm_x,
    ssm_bc,
    gate_z,
    conv_x,
    conv_bc,
    conv_prior_x,
    conv_prior_bc,
    step_dt,
    log_decay,
    skip_d,
    ssm_prior,
    norm_gain,
):
    vm = pl.BlockSpec(memory_space=pltpu.VMEM)
    anywhere = pl.BlockSpec(memory_space=pl.ANY)
    small = pl.BlockSpec(memory_space=pltpu.SMEM)
    return pl.pallas_call(
        kernel,
        out_shape=(
            jax.ShapeDtypeStruct((ROWS, WIDE), BF16),
            jax.ShapeDtypeStruct((ROWS, WIDE), BF16),
        ),
        in_specs=[vm] * 5 + [anywhere] + [vm] * 9 + [small, anywhere, vm],
        out_specs=(vm, vm),
        scratch_shapes=[
            pltpu.VMEM((2, CTX, 2, ROWS, HD), BF16),
            pltpu.VMEM((HEADS, ROWS, 2 * HD), F32),
            pltpu.VMEM((HEADS, ROWS, HD), F32),
            pltpu.VMEM((ROWS, TP * HEADS * HD), BF16),
            pltpu.VMEM((TP * HEADS * HD, WIDE), BF16),
            pltpu.VMEM((16, WIDE), BF16),
            pltpu.VMEM((16, 2 * NSTATE), BF16),
            pltpu.VMEM((2, ROWS + 8, 128), F32),
            pltpu.VMEM((ROWS + 8, 2 * NSTATE), F32),
            pltpu.VMEM((ROWS, NSTATE), BF16),
            pltpu.VMEM((ROWS, NSTATE), BF16),
            pltpu.VMEM((ROWS, ROWS), F32),
            pltpu.VMEM((ROWS, 128), F32),
            pltpu.VMEM((SH, ROWS), F32),
            pltpu.VMEM((ROWS, WIDE), F32),
            pltpu.VMEM((SH, MSG, NSTATE), BF16),
            pltpu.VMEM((SPOTS, MSG, NSTATE), BF16),
            pltpu.VMEM((SPOTS, MSG, NSTATE), BF16),
            pltpu.VMEM((SPOTS, MSG, NSTATE), BF16),
            pltpu.VMEM((64, NSTATE), F32),
            pltpu.VMEM((SPOTS, 64, NSTATE), BF16),
            pltpu.VMEM((SPOTS, 64, NSTATE), BF16),
            pltpu.VMEM((SPOTS * 64, NSTATE), BF16),
            pltpu.VMEM((WIDE, NSTATE), BF16),
            pltpu.VMEM((ROWS, 128), F32),
            pltpu.SemaphoreType.DMA,
            pltpu.SemaphoreType.DMA,
            pltpu.SemaphoreType.DMA((2,)),
            pltpu.SemaphoreType.DMA((2,)),
            pltpu.SemaphoreType.DMA((2, 10, 2, 2)),
            pltpu.SemaphoreType.DMA((CTX, 2, 2)),
            pltpu.SemaphoreType.DMA((2,)),
            pltpu.SemaphoreType.DMA((2,)),
            pltpu.SemaphoreType.DMA((4,)),
            pltpu.SemaphoreType.DMA((4,)),
            pltpu.SemaphoreType.DMA((SPOTS,)),
            pltpu.SemaphoreType.DMA((SPOTS,)),
            pltpu.SemaphoreType.DMA((SPOTS,)),
            pltpu.SemaphoreType.DMA((SPOTS,)),
            pltpu.SemaphoreType.DMA((4,)),
            pltpu.SemaphoreType.DMA((4,)),
            pltpu.SemaphoreType.DMA((HEADS, 3)),
            pltpu.SemaphoreType.DMA((TP, HEADS)),
        ],
        compiler_params=pltpu.CompilerParams(
            collective_id=0, has_side_effects=True, vmem_limit_bytes=60 * 2**20
        ),
        name="hybrid",
    )(
        queries,
        keys,
        values,
        prior_keys,
        prior_values,
        out_weight,
        ssm_x,
        ssm_bc.reshape(ROWS, 2 * NSTATE),
        gate_z,
        conv_x,
        conv_bc,
        conv_prior_x,
        conv_prior_bc,
        step_dt.T,
        log_decay.T,
        skip_d,
        ssm_prior.reshape(WIDE, NSTATE),
        norm_gain.reshape(1, WIDE),
    )


def solution(mesh):
    in_specs = (
        P("ctx", "tp"),
        P("ctx", "tp"),
        P("ctx", "tp"),
        P("ctx", "tp"),
        P("ctx", "tp"),
        P(None, "tp"),
        P("ctx", "tp"),
        P("ctx", None, "tp"),
        P("ctx", "tp"),
        P(None, "tp"),
        P(None, None, "tp"),
        P(None, "tp"),
        P(None, None, "tp"),
        P("ctx", "tp"),
        P("ctx", "tp"),
        P("tp"),
        P("tp", None, None),
        P("tp"),
    )
    out_specs = (P("ctx", "tp"), P("ctx", "tp"))
    return jax.shard_map(
        per_device, mesh=mesh, in_specs=in_specs, out_specs=out_specs, check_vma=False
    )
```
